128 devices in a mesh: ctx: 16 (over z_hi, y, core), head: 8 (over x, z_lo).
Axes of the slice: x: 4, y: 4, z: 4 (z_hi: 2, z_lo: 2; z = z_hi * 2 + z_lo), core: 2. Of those that a mesh axis runs over, the one named last changes fastest.
Arguments:
- queries: bfloat16 [4096, 5120], P('ctx', 'head'), may hold values from -6 to 6
- key_matrix_rows: bfloat16 [4096, 5120], P('ctx', 'head'), may hold values from -6 to 6
- value_matrix_rows: bfloat16 [4096, 5120], P('ctx', 'head'), may hold values from -6 to 6
- attention_output: bfloat16 [4096, 5120], P('ctx', 'head'), may hold values from -6 to 6
- output_gradient: bfloat16 [4096, 5120], P('ctx', 'head'), may hold values from -96 to 96
- log_sum_norm: float32 [40, 4096], P('head', 'ctx'), may hold values from 6 to 8
- features: bfloat16 [4096, 5120], P('ctx', 'head'), may hold values from -6 to 6
- adapter_down_weight: bfloat16 [3, 5120, 128], P(None, 'head'), may hold values from -0.078125 to 0.078125
- adapter_up_weight: bfloat16 [3, 128, 5120], P(None, None, 'head'), may hold values from -0.078125 to 0.078125
- attended_key_blocks: int32 [32, 16], P('ctx'), may hold values from 0 to 31, as said below
- used_block_count: int32 [32], P('ctx'), may hold values from 1 to 16, as said below
Outputs:
- query_grad: bfloat16 [4096, 5120], P('ctx', 'head')
- key_grad: bfloat16 [4096, 5120], P('ctx', 'head')
- value_grad: bfloat16 [4096, 5120], P('ctx', 'head')
- down_matrix_gradient: float32 [3, 5120, 128], P(None, 'head')
- up_matrix_gradient: float32 [3, 128, 5120], P(None, None, 'head')
The draws below stay inside these ranges and needn't reach their ends.
Inputs may be any that keep to these rules, and one draw needn't show every extreme that they name: `attended_key_blocks`: entries 0 to used_block_count[b] - 1 of row b are distinct, entry 0 is b itself, and the unused entries repeat entry 0. `used_block_count`: some row uses all 16 entries.
All inputs are finite; a program needn't handle non-finite values.
Results may differ from the reference program's by a relative error of at most 0.0058.
Values may be sent and summed in bfloat16 or wider, within the bound.
A program may use at most 64 MiB of HBM per device.

```python
import jax
import jax.numpy as jnp
from jax import lax

MODEL_WIDTH = 5120
ATTENTION_HEADS = 40
HEAD_WIDTH = 128
ADAPTER_RANK = 128
BLOCK = 128
FRAME = 12
MAXB = 16
TOKENS = 4096
NKB = 32


def mask_tables(key):
    first, second, third = jax.random.split(key, 3)
    blocks = jnp.arange(NKB, dtype=jnp.int32)
    frames = blocks // FRAME
    places = blocks % FRAME
    distance = 2 * jnp.abs(frames[:, None] - frames[None, :]) + jnp.abs(places[:, None] - places[None, :])
    noise = jax.random.randint(first, (NKB, NKB), 0, NKB, dtype=jnp.int32)
    priority = jnp.where(blocks[:, None] == blocks[None, :], -1, distance + noise)
    ranking = priority * NKB + blocks[None, :]
    ordered = jnp.argsort(ranking, axis=1, stable=True)[:, :MAXB].astype(jnp.int32)
    counts = jax.random.randint(second, (NKB,), 1, MAXB + 1, dtype=jnp.int32)
    fullrow = jax.random.randint(third, (), 0, NKB, dtype=jnp.int32)
    counts = jnp.where(blocks == fullrow, MAXB, counts).astype(jnp.int32)
    slots = jnp.arange(MAXB, dtype=jnp.int32)
    lists = jnp.where(slots[None, :] < counts[:, None], ordered, ordered[:, :1]).astype(jnp.int32)
    return (lists, counts)


def draw_attended_key_blocks(key, part):
    lists, counts = mask_tables(key)
    return lists


def draw_used_block_count(key, part):
    lists, counts = mask_tables(key)
    return counts


def levels(rng, extent, shards, smallest, high):
    level, own = 1.0, jax.random.fold_in(rng, 6)
    for position, parts in shards:
        heights = jnp.exp(jax.random.uniform(jax.random.fold_in(own, position), (parts,), jnp.float32, smallest / len(shards), high / len(shards)))
        level = level * jnp.repeat(heights, extent[position] // parts).reshape([-1 if axis == position else 1 for axis in range(len(extent))])
    return level


def centred(stream_key, extent, scale, limit, cuts=(), held_as=jnp.bfloat16):
    entries = scale * jax.random.normal(stream_key, extent, jnp.float32)
    if cuts:
        entries = entries * levels(stream_key, extent, cuts, -0.22, 0.18)
    return jnp.clip(entries, -limit, limit).astype(held_as)


def setup_inputs(seed: int = 0) -> dict:
    keys = jax.random.split(jax.random.key(seed), 12)
    queries = centred(keys[0], (TOKENS, ATTENTION_HEADS * HEAD_WIDTH), 1.0, 6.0, ((0, 16), (1, 8)))
    key_matrix_rows = centred(keys[1], (TOKENS, ATTENTION_HEADS * HEAD_WIDTH), 1.0, 6.0, ((0, 16), (1, 8)))
    value_matrix_rows = centred(keys[2], (TOKENS, ATTENTION_HEADS * HEAD_WIDTH), 1.0, 6.0, ((0, 16), (1, 8)))
    attention_output = centred(keys[3], (TOKENS, ATTENTION_HEADS * HEAD_WIDTH), 1.0, 6.0, ((0, 16), (1, 8)))
    output_gradient = centred(keys[4], (TOKENS, ATTENTION_HEADS * HEAD_WIDTH), 16.0, 96.0, ((0, 16), (1, 8)))
    log_sum_norm = jnp.clip(6.0 + 2.0 * jax.random.uniform(keys[5], (ATTENTION_HEADS, TOKENS), jnp.float32) ** levels(keys[5], (ATTENTION_HEADS, TOKENS), ((0, 8), (1, 16)), -0.2, 0.2), 6.0, 8.0)
    features = centred(keys[6], (TOKENS, MODEL_WIDTH), 1.0, 6.0, ((0, 16), (1, 8)))
    adapter_down_weight = centred(keys[7], (3, MODEL_WIDTH, ADAPTER_RANK), MODEL_WIDTH ** -0.5, 0.078125, ((1, 8),))
    adapter_up_weight = centred(keys[8], (3, ADAPTER_RANK, ATTENTION_HEADS * HEAD_WIDTH), (ATTENTION_HEADS * HEAD_WIDTH) ** -0.5, 0.078125, ((2, 8),))
    attended_key_blocks = draw_attended_key_blocks(jax.random.fold_in(keys[11], 71), 0)
    used_block_count = draw_used_block_count(jax.random.fold_in(keys[11], 71), 0)
    return dict(queries=queries, key_matrix_rows=key_matrix_rows, value_matrix_rows=value_matrix_rows, attention_output=attention_output, output_gradient=output_gradient, log_sum_norm=log_sum_norm, features=features, adapter_down_weight=adapter_down_weight, adapter_up_weight=adapter_up_weight, attended_key_blocks=attended_key_blocks, used_block_count=used_block_count)


adapter_scale = 0.125


def reference(queries, key_matrix_rows, value_matrix_rows, attention_output, output_gradient, log_sum_norm, features, adapter_down_weight, adapter_up_weight, attended_key_blocks, used_block_count):
    row_total = queries.shape[0]
    block_total = row_total // BLOCK
    scaling = HEAD_WIDTH ** -0.5
    query_blocks = queries.reshape(block_total, BLOCK, ATTENTION_HEADS, HEAD_WIDTH)
    key_blocks_all = key_matrix_rows.reshape(block_total, BLOCK, ATTENTION_HEADS, HEAD_WIDTH)
    value_blocks = value_matrix_rows.reshape(block_total, BLOCK, ATTENTION_HEADS, HEAD_WIDTH)
    grad_blocks = output_gradient.reshape(block_total, BLOCK, ATTENTION_HEADS, HEAD_WIDTH)
    row_dot = (output_gradient.astype(jnp.float32) * attention_output.astype(jnp.float32)).reshape(row_total, ATTENTION_HEADS, HEAD_WIDTH).sum(axis=2)
    dot_blocks = row_dot.reshape(block_total, BLOCK, ATTENTION_HEADS)
    norm_blocks = log_sum_norm.T.reshape(block_total, BLOCK, ATTENTION_HEADS)

    def one_block(carry, item):
        key_acc, value_acc = carry
        query_block, grad_block, norm_block, dot_block, chosen, used = item
        chosen = chosen.astype(jnp.int32)
        key_sel = key_blocks_all[chosen].reshape(MAXB * BLOCK, ATTENTION_HEADS, HEAD_WIDTH).astype(jnp.float32)
        value_sel = value_blocks[chosen].reshape(MAXB * BLOCK, ATTENTION_HEADS, HEAD_WIDTH).astype(jnp.float32)
        live_rows = jnp.repeat(jnp.arange(MAXB) < used, BLOCK, total_repeat_length=MAXB * BLOCK)
        query_f = query_block.astype(jnp.float32)
        grad_f = grad_block.astype(jnp.float32)
        scores = jnp.einsum("qhd,khd->hqk", query_f, key_sel)
        weights = jnp.where(live_rows[None, None, :], jnp.exp(scores * scaling - norm_block.T[:, :, None]), 0.0)
        weights_low = lax.optimization_barrier(weights.astype(jnp.bfloat16)).astype(jnp.float32)
        value_part = jnp.einsum("hqk,qhd->khd", weights_low, grad_f)
        value_dot = jnp.einsum("qhd,khd->hqk", grad_f, value_sel)
        score_grad = (weights * (value_dot - dot_block.T[:, :, None]) * scaling).astype(jnp.bfloat16)
        score_grad = lax.optimization_barrier(score_grad).astype(jnp.float32)
        query_part = jnp.einsum("hqk,khd->qhd", score_grad, key_sel)
        key_part = jnp.einsum("hqk,qhd->khd", score_grad, query_f)
        key_acc = key_acc.at[chosen].add(key_part.reshape(MAXB, BLOCK, ATTENTION_HEADS, HEAD_WIDTH))
        value_acc = value_acc.at[chosen].add(value_part.reshape(MAXB, BLOCK, ATTENTION_HEADS, HEAD_WIDTH))
        return (key_acc, value_acc), query_part.astype(jnp.bfloat16)

    start = jnp.zeros((block_total, BLOCK, ATTENTION_HEADS, HEAD_WIDTH), jnp.float32)
    (key_acc, value_acc), query_parts = lax.scan(one_block, (start, start), (query_blocks, grad_blocks, norm_blocks, dot_blocks, attended_key_blocks, used_block_count))
    query_grad = query_parts.reshape(row_total, ATTENTION_HEADS * HEAD_WIDTH)
    key_grad = key_acc.reshape(row_total, ATTENTION_HEADS * HEAD_WIDTH).astype(jnp.bfloat16)
    value_grad = value_acc.reshape(row_total, ATTENTION_HEADS * HEAD_WIDTH).astype(jnp.bfloat16)
    shifted_rows = jnp.stack([query_grad, key_grad, value_grad]).astype(jnp.float32)
    feature_rows_float = features.astype(jnp.float32)
    projected_rows = jnp.einsum("vc,fco->fvo", feature_rows_float, adapter_down_weight.astype(jnp.float32)).astype(jnp.bfloat16)
    projected_rows = lax.optimization_barrier(projected_rows).astype(jnp.float32)
    collected_rows = jnp.einsum("oki,oji->okj", shifted_rows, adapter_up_weight.astype(jnp.float32)).astype(jnp.bfloat16)
    collected_rows = lax.optimization_barrier(collected_rows).astype(jnp.float32)
    up_matrix_gradient = adapter_scale * jnp.einsum("pjf,pjd->pfd", projected_rows, shifted_rows)
    down_matrix_gradient = adapter_scale * jnp.einsum("sq,ysw->yqw", feature_rows_float, collected_rows)
    return (query_grad, key_grad, value_grad, down_matrix_gradient, up_matrix_gradient)
```

```python
import functools
import math

import jax
import jax.numpy as jnp
from jax import lax
from jax.experimental import pallas as pl
from jax.experimental.pallas import tpu as pltpu
from jax.sharding import PartitionSpec as P

MESH = pl.DeviceIdType.MESH
BF16 = jnp.bfloat16
F32 = jnp.float32

HEADS = 5
WIDTH = 128
TOKENS = 256
RING = 16
PARTS = 2
SPAN = RING // PARTS
KEYS = SPAN * TOKENS
TILE = 256
WORKERS = HEADS * PARTS
SCALE = WIDTH ** -0.5
LOG2E = math.log2(math.e)
DEAD = 1e30
adapter_scale = 0.125


def nt(a, b):
    return lax.dot_general(a, b, (((1,), (1,)), ((), ())), preferred_element_type=F32)


def nn(a, b):
    return lax.dot_general(a, b, (((1,), (0,)), ((), ())), preferred_element_type=F32)


def lane_slice(h):
    return pl.ds(pl.multiple_of(h * WIDTH, WIDTH), WIDTH)


def attention_kernel(
    q_ref, k_ref, v_ref, o_ref, g_ref, lse_ref, att_ref, used_ref,
    qg_ref, kg_ref, vg_ref,
    stats, rq, rg, rs, rk, rv, kt_buf, dk_acc, dv_acc, dq_acc,
    dqs, dks, dvs, rdq, rdk, rdv,
    q_send, g_send, s_send, k_send, v_send, dq_send, dk_send, dv_send,
    q_recv, g_recv, s_recv, k_recv, v_recv, dq_recv, dk_recv, dv_recv,
):
    me = lax.axis_index("ctx")
    group = lax.axis_index("head")

    def move(src, dst, send_sem, recv_sem, target):
        return pltpu.make_async_remote_copy(
            src_ref=src, dst_ref=dst, send_sem=send_sem, recv_sem=recv_sem,
            device_id=(target, group), device_id_type=MESH,
        )

    def start(src, dst, send_sem, recv_sem, target):
        @pl.when(target != me)
        def _():
            move(src, dst, send_sem, recv_sem, target).start()

        @pl.when(target == me)
        def _():
            pltpu.make_async_copy(src, dst, recv_sem).start()

    def sent(src, dst, send_sem, recv_sem, target):
        @pl.when(target != me)
        def _():
            move(src, dst, send_sem, recv_sem, target).wait_send()

    def landed(dst, recv_sem):
        pltpu.make_async_copy(dst, dst, recv_sem).wait()

    barrier = pltpu.get_barrier_semaphore()

    def greet(step, carry):
        pl.semaphore_signal(
            barrier, inc=1, device_id=(lax.rem(me + step, RING), group), device_id_type=MESH
        )
        return carry

    lax.fori_loop(1, RING, greet, 0)
    pl.semaphore_wait(barrier, RING - 1)

    my_part = me // SPAN
    my_place = lax.rem(me, SPAN)

    def kv_copies(h):
        target = h * PARTS + my_part
        rows = pl.ds(pl.multiple_of(my_place * TOKENS, TOKENS), TOKENS)
        return (
            (k_ref.at[:, lane_slice(h)], rk.at[rows], k_send.at[h], k_recv.at[my_place], target),
            (v_ref.at[:, lane_slice(h)], rv.at[rows], v_send.at[h], v_recv.at[my_place], target),
        )

    def send_kv(step, carry):
        h = lax.rem(step + me, HEADS)
        for copy in kv_copies(h):
            start(*copy)
        return carry

    lax.fori_loop(0, HEADS, send_kv, 0)

    lane = lax.broadcasted_iota(jnp.int32, (1, TOKENS), 1)
    codes = []
    for part in range(PARTS):
        words = []
        for row in range(2):
            word = jnp.int32(0)
            for slot in range(16):
                block = att_ref[row, slot] - part * 2 * SPAN
                inside = (block >= 0) & (block < 2 * SPAN) & (slot < used_ref[row])
                bit = jnp.left_shift(jnp.int32(1), jnp.clip(block, 0, 2 * SPAN - 1))
                word = word | jnp.where(inside, bit, 0)
            words.append(word)
        codes.append(jnp.where(lane < TOKENS // 2, words[0], words[1]).astype(F32))
    for h in range(HEADS):
        columns = slice(h * WIDTH, (h + 1) * WIDTH)
        product = g_ref[:, columns].astype(F32) * o_ref[:, columns].astype(F32)
        row_dot = jnp.sum(product.T, axis=0, keepdims=True)
        norm = lse_ref[h : h + 1, :] * LOG2E - math.log2(SCALE)
        for part in range(PARTS):
            stats[h * PARTS + part] = jnp.concatenate(
                [norm, row_dot, codes[part], jnp.zeros((5, TOKENS), F32)], axis=0
            )

    def query_copies(target):
        h = target // PARTS
        return (
            (stats.at[target], rs.at[me], s_send.at[target], s_recv.at[me], target),
            (q_ref.at[:, lane_slice(h)], rq.at[me], q_send.at[target], q_recv.at[me], target),
            (g_ref.at[:, lane_slice(h)], rg.at[me], g_send.at[target], g_recv.at[me], target),
        )

    def send_queries(step, carry):
        target = lax.rem(me + step, RING)

        @pl.when(target < WORKERS)
        def _():
            for copy in query_copies(target):
                start(*copy)

        return carry

    lax.fori_loop(0, RING, send_queries, 0)

    my_head = me // PARTS
    work_part = lax.rem(me, PARTS)

    def dq_copy(source):
        return (dqs.at[source], rdq.at[me], dq_send.at[source], dq_recv.at[me], source)

    def key_copies(place):
        target = work_part * SPAN + place
        rows = pl.ds(pl.multiple_of(place * TOKENS, TOKENS), TOKENS)
        return (
            (dks.at[rows], rdk.at[my_head], dk_send.at[place], dk_recv.at[my_head], target),
            (dvs.at[rows], rdv.at[my_head], dv_send.at[place], dv_recv.at[my_head], target),
        )

    @pl.when(me < WORKERS)
    def _work():
        def keys_in(place, carry):
            rows = pl.ds(pl.multiple_of(place * TOKENS, TOKENS), TOKENS)
            landed(rk.at[rows], k_recv.at[place])
            landed(rv.at[rows], v_recv.at[place])
            kt_buf[:, rows] = rk[rows].astype(F32).T.astype(BF16)
            dk_acc[rows] = jnp.zeros((TOKENS, WIDTH), F32)
            dv_acc[rows] = jnp.zeros((TOKENS, WIDTH), F32)
            return carry

        lax.fori_loop(0, SPAN, keys_in, 0)

        def one_source(step, carry):
            source = lax.rem(me - step + RING, RING)
            landed(rs.at[source], s_recv.at[source])
            landed(rq.at[source], q_recv.at[source])
            landed(rg.at[source], g_recv.at[source])
            queries = rq[source]
            grads = rg[source]
            norm = rs[source, 0:1, :]
            row_dot = rs[source, 1:2, :]
            code = rs[source, 2:3, :].astype(jnp.int32)
            dq_acc[...] = jnp.zeros_like(dq_acc)

            def one_tile(tile, inner):
                rows = pl.ds(pl.multiple_of(tile * TILE, TILE), TILE)
                keys = rk[rows]
                scores = nt(keys, queries)
                value_dot = nt(rv[rows], grads)
                low_parts, grad_parts = [], []
                for sub in range(TILE // 128):
                    bit = jnp.right_shift(code, tile * (TILE // 128) + sub) & 1
                    bias = jnp.where(bit > 0, norm, DEAD)
                    piece = slice(sub * 128, (sub + 1) * 128)
                    weights = jnp.exp2(scores[piece] * (SCALE * LOG2E) - bias)
                    low_parts.append(weights.astype(BF16))
                    grad_parts.append((weights * (value_dot[piece] - row_dot)).astype(BF16))
                low = jnp.concatenate(low_parts, axis=0)
                score_grad = jnp.concatenate(grad_parts, axis=0)
                dv_acc[rows] += nn(low, grads)
                dk_acc[rows] += nn(score_grad, queries)
                dq_acc[...] += nn(kt_buf[:, rows], score_grad)
                return inner

            lax.fori_loop(0, KEYS // TILE, one_tile, 0, unroll=2)
            dqs[source] = dq_acc[...].T.astype(BF16)
            start(*dq_copy(source))
            return carry

        lax.fori_loop(0, RING, one_source, 0)

        def keys_out(place, carry):
            rows = pl.ds(pl.multiple_of(place * TOKENS, TOKENS), TOKENS)
            dks[rows] = dk_acc[rows].astype(BF16)
            dvs[rows] = (dv_acc[rows] * (1.0 / SCALE)).astype(BF16)
            for copy in key_copies(place):
                start(*copy)
            return carry

        lax.fori_loop(0, SPAN, keys_out, 0)

    for h in range(HEADS):
        columns = slice(h * WIDTH, (h + 1) * WIDTH)
        total = None
        for part in range(PARTS):
            slot = h * PARTS + part
            landed(rdq.at[slot], dq_recv.at[slot])
            piece = rdq[slot].astype(F32)
            total = piece if total is None else total + piece
        qg_ref[:, columns] = total.astype(BF16)
    for h in range(HEADS):
        columns = slice(h * WIDTH, (h + 1) * WIDTH)
        landed(rdk.at[h], dk_recv.at[h])
        kg_ref[:, columns] = rdk[h]
        landed(rdv.at[h], dv_recv.at[h])
        vg_ref[:, columns] = rdv[h]

    def drain_kv(h, carry):
        for copy in kv_copies(h):
            sent(*copy)
        return carry

    lax.fori_loop(0, HEADS, drain_kv, 0)

    def drain_queries(target, carry):
        for copy in query_copies(target):
            sent(*copy)
        return carry

    lax.fori_loop(0, WORKERS, drain_queries, 0)

    @pl.when(me < WORKERS)
    def _drain():
        def drain_dq(source, carry):
            sent(*dq_copy(source))
            return carry

        lax.fori_loop(0, RING, drain_dq, 0)

        def drain_keys(place, carry):
            for copy in key_copies(place):
                sent(*copy)
            return carry

        lax.fori_loop(0, SPAN, drain_keys, 0)


def attention(queries, keys, values, output, grads, norm, blocks, used):
    vmem = pl.BlockSpec(memory_space=pltpu.VMEM)
    smem = pl.BlockSpec(memory_space=pltpu.SMEM)
    rows = jax.ShapeDtypeStruct((TOKENS, HEADS * WIDTH), BF16)
    dma = pltpu.SemaphoreType.DMA
    return pl.pallas_call(
        attention_kernel,
        out_shape=(rows, rows, rows),
        in_specs=[vmem] * 6 + [smem] * 2,
        out_specs=(vmem, vmem, vmem),
        scratch_shapes=[
            pltpu.VMEM((WORKERS, 8, TOKENS), F32),
            pltpu.VMEM((RING, TOKENS, WIDTH), BF16),
            pltpu.VMEM((RING, TOKENS, WIDTH), BF16),
            pltpu.VMEM((RING, 8, TOKENS), F32),
            pltpu.VMEM((KEYS, WIDTH), BF16),
            pltpu.VMEM((KEYS, WIDTH), BF16),
            pltpu.VMEM((WIDTH, KEYS), BF16),
            pltpu.VMEM((KEYS, WIDTH), F32),
            pltpu.VMEM((KEYS, WIDTH), F32),
            pltpu.VMEM((WIDTH, TOKENS), F32),
            pltpu.VMEM((RING, TOKENS, WIDTH), BF16),
            pltpu.VMEM((KEYS, WIDTH), BF16),
            pltpu.VMEM((KEYS, WIDTH), BF16),
            pltpu.VMEM((WORKERS, TOKENS, WIDTH), BF16),
            pltpu.VMEM((HEADS, TOKENS, WIDTH), BF16),
            pltpu.VMEM((HEADS, TOKENS, WIDTH), BF16),
            dma((WORKERS,)), dma((WORKERS,)), dma((WORKERS,)), dma((HEADS,)), dma((HEADS,)),
            dma((RING,)), dma((SPAN,)), dma((SPAN,)),
            dma((RING,)), dma((RING,)), dma((RING,)), dma((SPAN,)), dma((SPAN,)),
            dma((WORKERS,)), dma((HEADS,)), dma((HEADS,)),
        ],
        compiler_params=pltpu.CompilerParams(
            collective_id=0, has_side_effects=True, vmem_limit_bytes=48 * 2**20
        ),
        name="attention",
    )(queries, keys, values, output, grads, norm, blocks, used)


def on_device(
    queries,
    key_matrix_rows,
    value_matrix_rows,
    attention_output,
    output_gradient,
    log_sum_norm,
    features,
    adapter_down_weight,
    adapter_up_weight,
    attended_key_blocks,
    used_block_count,
):
    down_piece = jnp.einsum(
        "vc,fco->fvo", features, adapter_down_weight, preferred_element_type=jnp.float32
    )
    projected_rows = lax.psum(down_piece, "head").astype(jnp.bfloat16)
    query_grad, key_grad, value_grad = attention(
        queries, key_matrix_rows, value_matrix_rows, attention_output, output_gradient,
        log_sum_norm, attended_key_blocks, used_block_count,
    )
    shifted_rows = jnp.stack([query_grad, key_grad, value_grad])
    head_piece = jnp.einsum(
        "oki,oji->okj", shifted_rows, adapter_up_weight, preferred_element_type=jnp.float32
    )
    collected_rows = lax.psum(head_piece, "head").astype(jnp.bfloat16)
    up_piece = adapter_scale * jnp.einsum(
        "pjf,pjd->pfd", projected_rows, shifted_rows, preferred_element_type=jnp.float32
    )
    down_piece_gradient = adapter_scale * jnp.einsum(
        "sq,ysw->yqw", features, collected_rows, preferred_element_type=jnp.float32
    )
    down_matrix_gradient, up_matrix_gradient = lax.psum((down_piece_gradient, up_piece), "ctx")
    return (query_grad, key_grad, value_grad, down_matrix_gradient, up_matrix_gradient)


def solution(mesh):
    placed = (
        P("ctx", "head"),
        P("ctx", "head"),
        P("ctx", "head"),
        P("ctx", "head"),
        P("ctx", "head"),
        P("head", "ctx"),
        P("ctx", "head"),
        P(None, "head", None),
        P(None, None, "head"),
        P("ctx", None),
        P("ctx"),
    )
    return jax.shard_map(
        on_device,
        mesh=mesh,
        in_specs=placed,
        out_specs=(
            P("ctx", "head"),
            P("ctx", "head"),
            P("ctx", "head"),
            P(None, "head", None),
            P(None, None, "head"),
        ),
        check_vma=False,
    )
```

```python
import functools
import math

import jax
import jax.numpy as jnp
from jax import lax
from jax.experimental import pallas as pl
from jax.experimental.pallas import tpu as pltpu
from jax.sharding import PartitionSpec as P

MESH = pl.DeviceIdType.MESH
BF16 = jnp.bfloat16
F32 = jnp.float32

HEADS = 5
WIDTH = 128
TOKENS = 256
RING = 16
PARTS = 2
SPAN = RING // PARTS
KEYS = SPAN * TOKENS
TILE = 256
WORKERS = HEADS * PARTS
GROUPS = 8
SHARE = TOKENS // GROUPS
CHIPS = RING // 2
BLOCKS = 3 * HEADS
SCALE = WIDTH ** -0.5
LOG2E = math.log2(math.e)
DEAD = 1e30
adapter_scale = 0.125


def nt(a, b):
    return lax.dot_general(a, b, (((1,), (1,)), ((), ())), preferred_element_type=F32)


def nn(a, b):
    return lax.dot_general(a, b, (((1,), (0,)), ((), ())), preferred_element_type=F32)


def lane_slice(h):
    return pl.ds(pl.multiple_of(h * WIDTH, WIDTH), WIDTH)


def tn(a, b):
    return lax.dot_general(a, b, (((0,), (0,)), ((), ())), preferred_element_type=F32)


def layer_kernel(
    q_ref, k_ref, v_ref, o_ref, g_ref, lse_ref, f_ref, down_ref, up_ref, att_ref, used_ref,
    qg_ref, kg_ref, vg_ref, down_out, up_out,
    stats, rq, rg, rs, rk, rv, kt_buf, dk_acc, dv_acc, dq_acc,
    dqs, dks, dvs, rdq, rdk, rdv,
    q_send, g_send, s_send, k_send, v_send, dq_send, dk_send, dv_send,
    q_recv, g_recv, s_recv, k_recv, v_recv, dq_recv, dk_recv, dv_recv,
    row_send, row_land, row_all, row_sems,
    partial, pair_send, pair_land, sum_send, sum_land, total_all,
    pair_sems, sum_sems, total_sems, twin_sems,
):
    me = lax.axis_index("ctx")
    group = lax.axis_index("head")
    chip = me // 2
    core = lax.rem(me, 2)
    twin = me + 1 - 2 * core

    def move(src, dst, send_sem, recv_sem, target):
        return pltpu.make_async_remote_copy(
            src_ref=src, dst_ref=dst, send_sem=send_sem, recv_sem=recv_sem,
            device_id=(target, group), device_id_type=MESH,
        )

    def start(src, dst, send_sem, recv_sem, target):
        @pl.when(target != me)
        def _():
            move(src, dst, send_sem, recv_sem, target).start()

        @pl.when(target == me)
        def _():
            pltpu.make_async_copy(src, dst, recv_sem).start()

    def sent(src, dst, send_sem, recv_sem, target):
        @pl.when(target != me)
        def _():
            move(src, dst, send_sem, recv_sem, target).wait_send()

    def landed(dst, recv_sem):
        pltpu.make_async_copy(dst, dst, recv_sem).wait()

    barrier = pltpu.get_barrier_semaphore()

    def greet(step, carry):
        pl.semaphore_signal(
            barrier, inc=1, device_id=(lax.rem(me + step, RING), group), device_id_type=MESH
        )
        return carry

    def greet_head(step, carry):
        pl.semaphore_signal(
            barrier, inc=1, device_id=(me, lax.rem(group + step, GROUPS)), device_id_type=MESH
        )
        return carry

    lax.fori_loop(1, RING, greet, 0)
    lax.fori_loop(1, GROUPS, greet_head, 0)
    pl.semaphore_wait(barrier, RING + GROUPS - 2)

    def head_copy(kind, phase, other):
        if phase == 0:
            src, dst = row_send.at[kind, other], row_land.at[kind, group]
        else:
            src, dst = row_all.at[kind, group], row_all.at[kind, group]
        return pltpu.make_async_remote_copy(
            src_ref=src, dst_ref=dst,
            send_sem=row_sems.at[kind, phase, 0, other],
            recv_sem=row_sems.at[kind, phase, 1, group],
            device_id=(me, other), device_id_type=MESH,
        )

    def to_heads(kind, phase):
        def one(step, carry):
            head_copy(kind, phase, lax.rem(group + step, GROUPS)).start()
            return carry

        lax.fori_loop(1, GROUPS, one, 0)

    def from_heads(kind, phase):
        def one(step, carry):
            other = lax.rem(group + step, GROUPS)
            dst = (row_land if phase == 0 else row_all).at[kind, other]
            landed(dst, row_sems.at[kind, phase, 1, other])
            return carry

        lax.fori_loop(1, GROUPS, one, 0)

    def drain_heads(kind, phase):
        def one(step, carry):
            head_copy(kind, phase, lax.rem(group + step, GROUPS)).wait_send()
            return carry

        lax.fori_loop(1, GROUPS, one, 0)

    def split_rows(kind, m, rows):
        row_send[kind, :, m] = rows.astype(BF16).reshape(GROUPS, SHARE, WIDTH)

    def sum_rows(kind):
        row_land[kind, group] = row_send[kind, group]
        from_heads(kind, 0)
        row_all[kind, group] = jnp.sum(row_land[kind].astype(F32), axis=0).astype(BF16)
        to_heads(kind, 1)

    def all_rows(kind, m):
        return row_all[kind, :, m].reshape(TOKENS, WIDTH)

    my_part = me // SPAN
    my_place = lax.rem(me, SPAN)

    def kv_copies(h):
        target = h * PARTS + my_part
        rows = pl.ds(pl.multiple_of(my_place * TOKENS, TOKENS), TOKENS)
        return (
            (k_ref.at[:, lane_slice(h)], rk.at[rows], k_send.at[h], k_recv.at[my_place], target),
            (v_ref.at[:, lane_slice(h)], rv.at[rows], v_send.at[h], v_recv.at[my_place], target),
        )

    def send_kv(step, carry):
        h = lax.rem(step + me, HEADS)
        for copy in kv_copies(h):
            start(*copy)
        return carry

    lax.fori_loop(0, HEADS, send_kv, 0)

    lane = lax.broadcasted_iota(jnp.int32, (1, TOKENS), 1)
    codes = []
    for part in range(PARTS):
        words = []
        for row in range(2):
            word = jnp.int32(0)
            for slot in range(16):
                block = att_ref[row, slot] - part * 2 * SPAN
                inside = (block >= 0) & (block < 2 * SPAN) & (slot < used_ref[row])
                bit = jnp.left_shift(jnp.int32(1), jnp.clip(block, 0, 2 * SPAN - 1))
                word = word | jnp.where(inside, bit, 0)
            words.append(word)
        codes.append(jnp.where(lane < TOKENS // 2, words[0], words[1]).astype(F32))
    for h in range(HEADS):
        columns = slice(h * WIDTH, (h + 1) * WIDTH)
        product = g_ref[:, columns].astype(F32) * o_ref[:, columns].astype(F32)
        row_dot = jnp.sum(product.T, axis=0, keepdims=True)
        norm = lse_ref[h : h + 1, :] * LOG2E - math.log2(SCALE)
        for part in range(PARTS):
            stats[h * PARTS + part] = jnp.concatenate(
                [norm, row_dot, codes[part], jnp.zeros((5, TOKENS), F32)], axis=0
            )

    def query_copies(target):
        h = target // PARTS
        return (
            (stats.at[target], rs.at[me], s_send.at[target], s_recv.at[me], target),
            (q_ref.at[:, lane_slice(h)], rq.at[me], q_send.at[target], q_recv.at[me], target),
            (g_ref.at[:, lane_slice(h)], rg.at[me], g_send.at[target], g_recv.at[me], target),
        )

    def send_queries(step, carry):
        target = lax.rem(me + step, RING)

        @pl.when(target < WORKERS)
        def _():
            for copy in query_copies(target):
                start(*copy)

        return carry

    lax.fori_loop(0, RING, send_queries, 0)

    for m in range(3):
        split_rows(0, m, nn(f_ref[...], down_ref[m]))
    to_heads(0, 0)

    my_head = me // PARTS
    work_part = lax.rem(me, PARTS)

    def dq_copy(source):
        return (dqs.at[source], rdq.at[me], dq_send.at[source], dq_recv.at[me], source)

    def key_copies(place):
        target = work_part * SPAN + place
        rows = pl.ds(pl.multiple_of(place * TOKENS, TOKENS), TOKENS)
        return (
            (dks.at[rows], rdk.at[my_head], dk_send.at[place], dk_recv.at[my_head], target),
            (dvs.at[rows], rdv.at[my_head], dv_send.at[place], dv_recv.at[my_head], target),
        )

    def one_source(step, carry):
        source = lax.rem(me - step + RING, RING)
        landed(rs.at[source], s_recv.at[source])
        landed(rq.at[source], q_recv.at[source])
        landed(rg.at[source], g_recv.at[source])
        queries = rq[source]
        grads = rg[source]
        norm = rs[source, 0:1, :]
        row_dot = rs[source, 1:2, :]
        code = rs[source, 2:3, :].astype(jnp.int32)
        dq_acc[...] = jnp.zeros_like(dq_acc)

        def one_tile(tile, inner):
            rows = pl.ds(pl.multiple_of(tile * TILE, TILE), TILE)
            keys = rk[rows]
            scores = nt(keys, queries)
            value_dot = nt(rv[rows], grads)
            low_parts, grad_parts = [], []
            for sub in range(TILE // 128):
                bit = jnp.right_shift(code, tile * (TILE // 128) + sub) & 1
                bias = jnp.where(bit > 0, norm, DEAD)
                piece = slice(sub * 128, (sub + 1) * 128)
                weights = jnp.exp2(scores[piece] * (SCALE * LOG2E) - bias)
                low_parts.append(weights.astype(BF16))
                grad_parts.append((weights * (value_dot[piece] - row_dot)).astype(BF16))
            low = jnp.concatenate(low_parts, axis=0)
            score_grad = jnp.concatenate(grad_parts, axis=0)
            dv_acc[rows] += nn(low, grads)
            dk_acc[rows] += nn(score_grad, queries)
            dq_acc[...] += nn(kt_buf[:, rows], score_grad)
            return inner

        lax.fori_loop(0, KEYS // TILE, one_tile, 0, unroll=2)
        dqs[source] = dq_acc[...].T.astype(BF16)
        start(*dq_copy(source))
        return carry

    @pl.when(me < WORKERS)
    def _work():
        def keys_in(place, carry):
            rows = pl.ds(pl.multiple_of(place * TOKENS, TOKENS), TOKENS)
            landed(rk.at[rows], k_recv.at[place])
            landed(rv.at[rows], v_recv.at[place])
            kt_buf[:, rows] = rk[rows].astype(F32).T.astype(BF16)
            dk_acc[rows] = jnp.zeros((TOKENS, WIDTH), F32)
            dv_acc[rows] = jnp.zeros((TOKENS, WIDTH), F32)
            return carry

        lax.fori_loop(0, SPAN, keys_in, 0)

        lax.fori_loop(0, RING // 2, one_source, 0)

    sum_rows(0)

    @pl.when(me < WORKERS)
    def _more_work():
        lax.fori_loop(RING // 2, RING, one_source, 0)

        def keys_out(place, carry):
            rows = pl.ds(pl.multiple_of(place * TOKENS, TOKENS), TOKENS)
            dks[rows] = dk_acc[rows].astype(BF16)
            dvs[rows] = (dv_acc[rows] * (1.0 / SCALE)).astype(BF16)
            for copy in key_copies(place):
                start(*copy)
            return carry

        lax.fori_loop(0, SPAN, keys_out, 0)

    for h in range(HEADS):
        columns = slice(h * WIDTH, (h + 1) * WIDTH)
        total = None
        for part in range(PARTS):
            slot = h * PARTS + part
            landed(rdq.at[slot], dq_recv.at[slot])
            piece = rdq[slot].astype(F32)
            total = piece if total is None else total + piece
        qg_ref[:, columns] = total.astype(BF16)
    for h in range(HEADS):
        columns = slice(h * WIDTH, (h + 1) * WIDTH)
        landed(rdk.at[h], dk_recv.at[h])
        kg_ref[:, columns] = rdk[h]
        landed(rdv.at[h], dv_recv.at[h])
        vg_ref[:, columns] = rdv[h]
    from_heads(0, 1)

    grads_out = (qg_ref, kg_ref, vg_ref)
    for m in range(3):
        split_rows(1, m, nt(grads_out[m][...], up_ref[m]))
    to_heads(1, 0)

    twin_copy = pltpu.make_async_remote_copy(
        src_ref=pair_send, dst_ref=pair_land, send_sem=pair_sems.at[0], recv_sem=pair_sems.at[1],
        device_id=(twin, group), device_id_type=MESH,
    )

    def chip_at(step):
        return lax.rem(chip + step, CHIPS)

    def sum_copy(other):
        return pltpu.make_async_remote_copy(
            src_ref=sum_send.at[other], dst_ref=sum_land.at[chip],
            send_sem=sum_sems.at[0, other], recv_sem=sum_sems.at[1, chip],
            device_id=(2 * other + core, group), device_id_type=MESH,
        )

    def total_copy(other):
        return pltpu.make_async_remote_copy(
            src_ref=total_all.at[core, chip], dst_ref=total_all.at[core, chip],
            send_sem=total_sems.at[0, other], recv_sem=total_sems.at[1, chip],
            device_id=(2 * other + core, group), device_id_type=MESH,
        )

    def pass_copy(origin):
        return pltpu.make_async_remote_copy(
            src_ref=total_all.at[core, origin], dst_ref=total_all.at[core, origin],
            send_sem=twin_sems.at[0, origin], recv_sem=twin_sems.at[1, origin],
            device_id=(twin, group), device_id_type=MESH,
        )

    def hand_over():
        for block in range(BLOCKS):
            pair_send[block] = partial[block].astype(BF16)
        twin_copy.start()

    def take_over():
        twin_copy.wait_recv()
        for block in range(BLOCKS):
            both = partial[block] + pair_land[block].astype(F32)
            sum_send[block // 2, block % 2] = both.astype(BF16)
        sum_send[CHIPS - 1, 1] = jnp.zeros((WIDTH, WIDTH), BF16)
        for step in range(1, CHIPS):
            sum_copy(chip_at(step)).start()
        sum_land[chip] = sum_send[chip]

    for m in range(3):
        rows = tn(all_rows(0, m), grads_out[m][...]) * adapter_scale
        for h in range(HEADS):
            partial[m * HEADS + h] = rows[:, h * WIDTH : (h + 1) * WIDTH]
    pl.when(core == 1)(hand_over)
    sum_rows(1)
    pl.when(core == 0)(take_over)
    from_heads(1, 1)

    @pl.when(core == 0)
    def _down_over():
        for m in range(3):
            rows = tn(f_ref[...], all_rows(1, m)) * adapter_scale
            for h in range(HEADS):
                pair_send[m * HEADS + h] = rows[h * WIDTH : (h + 1) * WIDTH].astype(BF16)
        twin_copy.start()

    @pl.when(core == 1)
    def _down_sum():
        for m in range(3):
            rows = tn(f_ref[...], all_rows(1, m)) * adapter_scale
            for h in range(HEADS):
                partial[m * HEADS + h] = rows[h * WIDTH : (h + 1) * WIDTH]
        take_over()

    for step in range(1, CHIPS):
        other = chip_at(step)
        landed(sum_land.at[other], sum_sems.at[1, other])
    total_all[core, chip] = jnp.sum(sum_land[...].astype(F32), axis=0).astype(BF16)
    for step in range(1, CHIPS):
        total_copy(chip_at(step)).start()
    pass_copy(chip).start()
    for step in range(1, CHIPS):
        other = chip_at(step)
        landed(total_all.at[core, other], total_sems.at[1, other])
        pass_copy(other).start()
    for origin in range(CHIPS):
        landed(total_all.at[1 - core, origin], twin_sems.at[1, origin])
    for block in range(BLOCKS):
        m, h = block // HEADS, block % HEADS
        columns = slice(h * WIDTH, (h + 1) * WIDTH)
        up_out[m, :, columns] = total_all[0, block // 2, block % 2].astype(F32)
        down_out[m, columns, :] = total_all[1, block // 2, block % 2].astype(F32)

    for kind in range(2):
        for phase in range(2):
            drain_heads(kind, phase)
    twin_copy.wait_send()
    for step in range(1, CHIPS):
        sum_copy(chip_at(step)).wait_send()
        total_copy(chip_at(step)).wait_send()
    for origin in range(CHIPS):
        pass_copy(origin).wait_send()

    def drain_kv(h, carry):
        for copy in kv_copies(h):
            sent(*copy)
        return carry

    lax.fori_loop(0, HEADS, drain_kv, 0)

    def drain_queries(target, carry):
        for copy in query_copies(target):
            sent(*copy)
        return carry

    lax.fori_loop(0, WORKERS, drain_queries, 0)

    @pl.when(me < WORKERS)
    def _drain():
        def drain_dq(source, carry):
            sent(*dq_copy(source))
            return carry

        lax.fori_loop(0, RING, drain_dq, 0)

        def drain_keys(place, carry):
            for copy in key_copies(place):
                sent(*copy)
            return carry

        lax.fori_loop(0, SPAN, drain_keys, 0)


def on_device(
    queries,
    key_matrix_rows,
    value_matrix_rows,
    attention_output,
    output_gradient,
    log_sum_norm,
    features,
    adapter_down_weight,
    adapter_up_weight,
    attended_key_blocks,
    used_block_count,
):
    vmem = pl.BlockSpec(memory_space=pltpu.VMEM)
    smem = pl.BlockSpec(memory_space=pltpu.SMEM)
    rows = jax.ShapeDtypeStruct((TOKENS, HEADS * WIDTH), BF16)
    down = jax.ShapeDtypeStruct((3, HEADS * WIDTH, WIDTH), F32)
    up = jax.ShapeDtypeStruct((3, WIDTH, HEADS * WIDTH), F32)
    dma = pltpu.SemaphoreType.DMA
    return pl.pallas_call(
        layer_kernel,
        out_shape=(rows, rows, rows, down, up),
        in_specs=[vmem] * 9 + [smem] * 2,
        out_specs=(vmem,) * 5,
        scratch_shapes=[
            pltpu.VMEM((WORKERS, 8, TOKENS), F32),
            pltpu.VMEM((RING, TOKENS, WIDTH), BF16),
            pltpu.VMEM((RING, TOKENS, WIDTH), BF16),
            pltpu.VMEM((RING, 8, TOKENS), F32),
            pltpu.VMEM((KEYS, WIDTH), BF16),
            pltpu.VMEM((KEYS, WIDTH), BF16),
            pltpu.VMEM((WIDTH, KEYS), BF16),
            pltpu.VMEM((KEYS, WIDTH), F32),
            pltpu.VMEM((KEYS, WIDTH), F32),
            pltpu.VMEM((WIDTH, TOKENS), F32),
            pltpu.VMEM((RING, TOKENS, WIDTH), BF16),
            pltpu.VMEM((KEYS, WIDTH), BF16),
            pltpu.VMEM((KEYS, WIDTH), BF16),
            pltpu.VMEM((WORKERS, TOKENS, WIDTH), BF16),
            pltpu.VMEM((HEADS, TOKENS, WIDTH), BF16),
            pltpu.VMEM((HEADS, TOKENS, WIDTH), BF16),
            dma((WORKERS,)), dma((WORKERS,)), dma((WORKERS,)), dma((HEADS,)), dma((HEADS,)),
            dma((RING,)), dma((SPAN,)), dma((SPAN,)),
            dma((RING,)), dma((RING,)), dma((RING,)), dma((SPAN,)), dma((SPAN,)),
            dma((WORKERS,)), dma((HEADS,)), dma((HEADS,)),
            pltpu.VMEM((2, GROUPS, 3, SHARE, WIDTH), BF16),
            pltpu.VMEM((2, GROUPS, 3, SHARE, WIDTH), BF16),
            pltpu.VMEM((2, GROUPS, 3, SHARE, WIDTH), BF16),
            dma((2, 2, 2, GROUPS)),
            pltpu.VMEM((BLOCKS, WIDTH, WIDTH), F32),
            pltpu.VMEM((BLOCKS, WIDTH, WIDTH), BF16),
            pltpu.VMEM((BLOCKS, WIDTH, WIDTH), BF16),
            pltpu.VMEM((CHIPS, 2, WIDTH, WIDTH), BF16),
            pltpu.VMEM((CHIPS, 2, WIDTH, WIDTH), BF16),
            pltpu.VMEM((2, CHIPS, 2, WIDTH, WIDTH), BF16),
            dma((2,)), dma((2, CHIPS)), dma((2, CHIPS)), dma((2, CHIPS)),
        ],
        compiler_params=pltpu.CompilerParams(
            collective_id=0, has_side_effects=True, vmem_limit_bytes=48 * 2**20
        ),
        name="layer",
    )(
        queries, key_matrix_rows, value_matrix_rows, attention_output, output_gradient,
        log_sum_norm, features, adapter_down_weight, adapter_up_weight,
        attended_key_blocks, used_block_count,
    )


def solution(mesh):
    placed = (
        P("ctx", "head"),
        P("ctx", "head"),
        P("ctx", "head"),
        P("ctx", "head"),
        P("ctx", "head"),
        P("head", "ctx"),
        P("ctx", "head"),
        P(None, "head", None),
        P(None, None, "head"),
        P("ctx", None),
        P("ctx"),
    )
    return jax.shard_map(
        on_device,
        mesh=mesh,
        in_specs=placed,
        out_specs=(
            P("ctx", "head"),
            P("ctx", "head"),
            P("ctx", "head"),
            P(None, "head", None),
            P(None, None, "head"),
        ),
        check_vma=False,
    )
```

```python
import functools
import math

import jax
import jax.numpy as jnp
from jax import lax
from jax.experimental import pallas as pl
from jax.experimental.pallas import tpu as pltpu
from jax.sharding import PartitionSpec as P

MESH = pl.DeviceIdType.MESH
BF16 = jnp.bfloat16
F32 = jnp.float32

HEADS = 5
WIDTH = 128
TOKENS = 256
RING = 16
BLOCK = 128
GROUPS = 8
SHARE = TOKENS // GROUPS
CHIPS = RING // 2
BLOCKS = 3 * HEADS
SCALE = WIDTH ** -0.5
LOG2E = math.log2(math.e)
DEAD = 1e30
adapter_scale = 0.125


def nt(a, b):
    return lax.dot_general(a, b, (((1,), (1,)), ((), ())), preferred_element_type=F32)


def nn(a, b):
    return lax.dot_general(a, b, (((1,), (0,)), ((), ())), preferred_element_type=F32)


def lane_slice(h):
    return pl.ds(pl.multiple_of(h * WIDTH, WIDTH), WIDTH)


def tn(a, b):
    return lax.dot_general(a, b, (((0,), (0,)), ((), ())), preferred_element_type=F32)


def layer_kernel(
    q_ref, k_ref, v_ref, o_ref, g_ref, lse_ref, f_ref, down_ref, up_ref, att_ref, used_ref,
    qg_ref, kg_ref, vg_ref, down_out, up_out,
    o_here, g_here, lse_here, f_here, down_here, up_here, in_sems,
    stats, rs, rqg, rkv, keys_t, dk_acc, dv_acc, dq_acc, dq_land, dq_out, dkv_out, rdq, rdkv,
    s_send, qg_send, kv_send, pass_send, dq_pair_send, dq_send, dkv_send,
    s_recv, qg_recv, kv_recv, pass_recv, dq_pair_recv, dq_recv, dkv_recv,
    row_send, row_land, row_all, row_sems,
    partial, pair_send, pair_land, sum_send, sum_land, total_all,
    pair_sems, sum_sems, total_sems, twin_sems,
):
    me = lax.axis_index("ctx")
    group = lax.axis_index("head")
    chip = me // 2
    core = lax.rem(me, 2)
    twin = me + 1 - 2 * core

    def chip_at(step):
        return lax.rem(chip + step, CHIPS)

    def move(src, dst, send_sem, recv_sem, target):
        return pltpu.make_async_remote_copy(
            src_ref=src, dst_ref=dst, send_sem=send_sem, recv_sem=recv_sem,
            device_id=(target, group), device_id_type=MESH,
        )

    def start(src, dst, send_sem, recv_sem, target):
        @pl.when(target != me)
        def _():
            move(src, dst, send_sem, recv_sem, target).start()

        @pl.when(target == me)
        def _():
            pltpu.make_async_copy(src, dst, recv_sem).start()

    def sent(src, dst, send_sem, recv_sem, target):
        @pl.when(target != me)
        def _():
            move(src, dst, send_sem, recv_sem, target).wait_send()

    def landed(dst, recv_sem):
        pltpu.make_async_copy(dst, dst, recv_sem).wait()

    barrier = pltpu.get_barrier_semaphore()

    def greet(step, carry):
        pl.semaphore_signal(
            barrier, inc=1, device_id=(2 * chip_at(step) + core, group), device_id_type=MESH
        )
        return carry

    def greet_head(step, carry):
        pl.semaphore_signal(
            barrier, inc=1, device_id=(me, lax.rem(group + step, GROUPS)), device_id_type=MESH
        )
        return carry

    pl.semaphore_signal(barrier, inc=1, device_id=(twin, group), device_id_type=MESH)
    lax.fori_loop(1, CHIPS, greet, 0)
    lax.fori_loop(1, GROUPS, greet_head, 0)

    inputs = [
        pltpu.make_async_copy(src, dst, in_sems.at[index])
        for index, (src, dst) in enumerate(
            (
                (g_ref, g_here), (o_ref, o_here), (lse_ref, lse_here),
                (f_ref, f_here), (down_ref, down_here), (up_ref, up_here),
            )
        )
    ]
    for copy in inputs:
        copy.start()

    lane = lax.broadcasted_iota(jnp.int32, (1, TOKENS), 1)
    words = [[jnp.int32(0), jnp.int32(0)], [jnp.int32(0), jnp.int32(0)]]
    for row in range(2):
        for slot in range(16):
            block = att_ref[row, slot]
            owner = jnp.right_shift(block, 1)
            bit = jnp.left_shift(jnp.int32(1), jnp.right_shift(block, 2) * 2 + (block & 1))
            for part in range(2):
                inside = ((owner & 1) == part) & (slot < used_ref[row])
                words[part][row] = words[part][row] | jnp.where(inside, bit, 0)
    codes = [
        jnp.where(lane < TOKENS // 2, word[0], word[1]).astype(F32) for word in words
    ]
    for copy in inputs[:3]:
        copy.wait()
    for h in range(HEADS):
        columns = slice(h * WIDTH, (h + 1) * WIDTH)
        product = g_here[:, columns].astype(F32) * o_here[:, columns].astype(F32)
        row_dot = jnp.sum(product.T, axis=0, keepdims=True)
        norm = lse_here[h : h + 1, :] * LOG2E
        stats[h] = jnp.concatenate(
            [norm, row_dot, codes[0], codes[1], jnp.zeros((4, TOKENS), F32)], axis=0
        )

    pl.semaphore_wait(barrier, CHIPS + GROUPS - 1)

    def query_copies(h):
        target = 2 * lax.rem(5 * h, CHIPS) + core
        lanes = lane_slice(h)
        return (
            (stats.at[h], rs.at[chip, core], s_send.at[h], s_recv.at[chip], target),
            (q_ref.at[:, lanes], rqg.at[chip, core, 0], qg_send.at[0, h], qg_recv.at[chip], target),
            (g_ref.at[:, lanes], rqg.at[chip, core, 1], qg_send.at[1, h], qg_recv.at[chip], target),
        )

    def key_copies(h):
        target = 2 * lax.rem(5 * h, CHIPS) + core
        lanes = lane_slice(h)
        return (
            (k_ref.at[:, lanes], rkv.at[chip, 0], kv_send.at[0, h], kv_recv.at[chip], target),
            (v_ref.at[:, lanes], rkv.at[chip, 1], kv_send.at[1, h], kv_recv.at[chip], target),
        )

    def send_all(copies):
        def one(step, carry):
            h = lax.rem(5 * lax.rem(chip - step + CHIPS, CHIPS), CHIPS)

            @pl.when(h < HEADS)
            def _():
                for copy in copies(h):
                    start(*copy)

            return carry

        lax.fori_loop(0, CHIPS, one, 0)

    send_all(query_copies)
    send_all(key_copies)

    def head_copy(kind, phase, other):
        if phase == 0:
            src, dst = row_send.at[kind, other], row_land.at[kind, group]
        else:
            src, dst = row_all.at[kind, group], row_all.at[kind, group]
        return pltpu.make_async_remote_copy(
            src_ref=src, dst_ref=dst,
            send_sem=row_sems.at[kind, phase, 0, other],
            recv_sem=row_sems.at[kind, phase, 1, group],
            device_id=(me, other), device_id_type=MESH,
        )

    def to_heads(kind, phase):
        def one(step, carry):
            head_copy(kind, phase, lax.rem(group + step, GROUPS)).start()
            return carry

        lax.fori_loop(1, GROUPS, one, 0)

    def from_heads(kind, phase):
        def one(step, carry):
            other = lax.rem(group + step, GROUPS)
            dst = (row_land if phase == 0 else row_all).at[kind, other]
            landed(dst, row_sems.at[kind, phase, 1, other])
            return carry

        lax.fori_loop(1, GROUPS, one, 0)

    def drain_heads(kind, phase):
        def one(step, carry):
            head_copy(kind, phase, lax.rem(group + step, GROUPS)).wait_send()
            return carry

        lax.fori_loop(1, GROUPS, one, 0)

    def split_rows(kind, m, rows):
        row_send[kind, :, m] = rows.astype(BF16).reshape(GROUPS, SHARE, WIDTH)

    def sum_rows(kind):
        row_land[kind, group] = row_send[kind, group]
        from_heads(kind, 0)
        row_all[kind, group] = jnp.sum(row_land[kind].astype(F32), axis=0).astype(BF16)
        to_heads(kind, 1)

    def all_rows(kind, m):
        return row_all[kind, :, m].reshape(TOKENS, WIDTH)

    inputs[3].wait()
    inputs[4].wait()
    for m in range(3):
        split_rows(0, m, nn(f_here[...], down_here[m]))
    to_heads(0, 0)

    my_head = lax.rem(5 * chip, CHIPS)
    working = my_head < HEADS

    def pass_copies(origin):
        return (
            (rs.at[origin, core], rs.at[origin, core],
             pass_send.at[0, origin], pass_recv.at[0, origin], twin),
            (rqg.at[origin, core], rqg.at[origin, core],
             pass_send.at[1, origin], pass_recv.at[1, origin], twin),
        )

    def dq_pair_copy(origin):
        return (dq_acc.at[origin, 1 - core], dq_land.at[origin],
                dq_pair_send.at[origin], dq_pair_recv.at[origin], twin)

    def dq_copy(origin):
        return (dq_out.at[origin], rdq.at[my_head],
                dq_send.at[origin], dq_recv.at[my_head], 2 * origin + core)

    def dkv_copy(origin):
        return (dkv_out.at[origin], rdkv.at[my_head],
                dkv_send.at[origin], dkv_recv.at[my_head], 2 * origin + core)

    def compute(key_chip, origin, first):
        keys = rkv[key_chip, 0]
        queries = rqg[origin, :, 0].reshape(2 * TOKENS, WIDTH)
        grads = rqg[origin, :, 1].reshape(2 * TOKENS, WIDTH)
        norm = jnp.concatenate([rs[origin, side, 0:1, :] for side in range(2)], axis=1)
        row_dot = jnp.concatenate([rs[origin, side, 1:2, :] for side in range(2)], axis=1)
        code = jnp.concatenate(
            [
                jnp.where(core == 0, rs[origin, side, 2:3, :], rs[origin, side, 3:4, :])
                for side in range(2)
            ],
            axis=1,
        ).astype(jnp.int32)
        scores = nt(keys, queries)
        value_dot = nt(rkv[key_chip, 1], grads)
        low_parts, grad_parts = [], []
        for sub in range(2):
            bit = jnp.right_shift(code, key_chip * 2 + sub) & 1
            bias = jnp.where(bit > 0, norm, DEAD)
            piece = slice(sub * BLOCK, (sub + 1) * BLOCK)
            weights = jnp.exp2(scores[piece] * (SCALE * LOG2E) - bias)
            low_parts.append(weights.astype(BF16))
            grad_parts.append(
                (weights * ((value_dot[piece] - row_dot) * SCALE)).astype(BF16)
            )
        low = jnp.concatenate(low_parts, axis=0)
        score_grad = jnp.concatenate(grad_parts, axis=0)
        dv_acc[...] += nn(low, grads)
        dk_acc[...] += nn(score_grad, queries)
        dq_part = nn(keys_t[...], score_grad)
        for side in range(2):
            piece = dq_part[:, side * TOKENS : (side + 1) * TOKENS]
            if first:
                dq_acc[origin, side] = piece
            else:
                dq_acc[origin, side] += piece

    def open_keys(key_chip):
        landed(rkv.at[key_chip], kv_recv.at[key_chip])
        keys_t[...] = rkv[key_chip, 0].astype(F32).T.astype(BF16)
        dk_acc[...] = jnp.zeros_like(dk_acc)
        dv_acc[...] = jnp.zeros_like(dv_acc)

    def close_keys(key_chip):
        dkv_out[key_chip, 0] = dk_acc[...].astype(BF16)
        dkv_out[key_chip, 1] = dv_acc[...].astype(BF16)
        start(*dkv_copy(key_chip))

    @pl.when(working)
    def _first_keys():
        open_keys(chip)

        def receive(step, carry):
            origin = chip_at(step)
            landed(rs.at[origin, core], s_recv.at[origin])
            landed(rqg.at[origin, core], qg_recv.at[origin])
            for copy in pass_copies(origin):
                move(*copy).start()
            return carry

        def use(step, carry):
            origin = chip_at(step)
            landed(rs.at[origin, 1 - core], pass_recv.at[0, origin])
            landed(rqg.at[origin, 1 - core], pass_recv.at[1, origin])
            compute(chip, origin, True)
            return carry

        receive(0, 0)

        def both(step, carry):
            receive(step, carry)
            return use(step - 1, carry)

        lax.fori_loop(1, CHIPS, both, 0)
        use(CHIPS - 1, 0)
        close_keys(chip)

    sum_rows(0)

    @pl.when(working)
    def _other_keys():
        def middle(turn, carry):
            key_chip = chip_at(turn)
            open_keys(key_chip)

            def one(step, inner):
                compute(key_chip, chip_at(step), False)
                return inner

            lax.fori_loop(0, CHIPS, one, 0)
            close_keys(key_chip)
            return carry

        lax.fori_loop(1, CHIPS - 1, middle, 0)

        key_chip = chip_at(CHIPS - 1)
        open_keys(key_chip)

        def finish(step):
            origin = chip_at(step)
            landed(dq_land.at[origin], dq_pair_recv.at[origin])
            total = dq_acc[origin, core] + dq_land[origin]
            dq_out[origin] = total.T.astype(BF16)
            start(*dq_copy(origin))

        def last(step, carry):
            origin = chip_at(step)
            compute(key_chip, origin, False)
            move(*dq_pair_copy(origin)).start()

            @pl.when(step > 0)
            def _():
                finish(step - 1)

            return carry

        lax.fori_loop(0, CHIPS, last, 0)
        close_keys(key_chip)
        finish(CHIPS - 1)

    for h in range(HEADS):
        columns = slice(h * WIDTH, (h + 1) * WIDTH)
        landed(rdkv.at[h], dkv_recv.at[h])
        kg_ref[:, columns] = rdkv[h, 0]
        vg_ref[:, columns] = rdkv[h, 1]
    from_heads(0, 1)
    inputs[5].wait()

    grads_out = (qg_ref, kg_ref, vg_ref)

    def gather_rows(m):
        split_rows(1, m, nt(grads_out[m][...], up_here[m]))

    def up_rows(m):
        rows = tn(all_rows(0, m), grads_out[m][...]) * adapter_scale
        for h in range(HEADS):
            partial[m * HEADS + h] = rows[:, h * WIDTH : (h + 1) * WIDTH]

    for m in (1, 2):
        gather_rows(m)
        up_rows(m)
    for h in range(HEADS):
        landed(rdq.at[h], dq_recv.at[h])
        qg_ref[:, h * WIDTH : (h + 1) * WIDTH] = rdq[h]
    gather_rows(0)
    to_heads(1, 0)
    up_rows(0)

    twin_copy = pltpu.make_async_remote_copy(
        src_ref=pair_send, dst_ref=pair_land, send_sem=pair_sems.at[0], recv_sem=pair_sems.at[1],
        device_id=(twin, group), device_id_type=MESH,
    )

    def sum_copy(other):
        return pltpu.make_async_remote_copy(
            src_ref=sum_send.at[other], dst_ref=sum_land.at[chip],
            send_sem=sum_sems.at[0, other], recv_sem=sum_sems.at[1, chip],
            device_id=(2 * other + core, group), device_id_type=MESH,
        )

    def total_copy(other):
        return pltpu.make_async_remote_copy(
            src_ref=total_all.at[core, chip], dst_ref=total_all.at[core, chip],
            send_sem=total_sems.at[0, other], recv_sem=total_sems.at[1, chip],
            device_id=(2 * other + core, group), device_id_type=MESH,
        )

    def pass_copy(origin):
        return pltpu.make_async_remote_copy(
            src_ref=total_all.at[core, origin], dst_ref=total_all.at[core, origin],
            send_sem=twin_sems.at[0, origin], recv_sem=twin_sems.at[1, origin],
            device_id=(twin, group), device_id_type=MESH,
        )

    def hand_over():
        for block in range(BLOCKS):
            pair_send[block] = partial[block].astype(BF16)
        twin_copy.start()

    def take_over():
        twin_copy.wait_recv()
        for block in range(BLOCKS):
            both = partial[block] + pair_land[block].astype(F32)
            sum_send[block // 2, block % 2] = both.astype(BF16)
        sum_send[CHIPS - 1, 1] = jnp.zeros((WIDTH, WIDTH), BF16)
        for step in range(1, CHIPS):
            sum_copy(chip_at(step)).start()
        sum_land[chip] = sum_send[chip]

    pl.when(core == 1)(hand_over)
    sum_rows(1)
    pl.when(core == 0)(take_over)
    from_heads(1, 1)

    @pl.when(core == 0)
    def _down_over():
        for m in range(3):
            rows = tn(f_here[...], all_rows(1, m)) * adapter_scale
            for h in range(HEADS):
                pair_send[m * HEADS + h] = rows[h * WIDTH : (h + 1) * WIDTH].astype(BF16)
        twin_copy.start()

    @pl.when(core == 1)
    def _down_sum():
        for m in range(3):
            rows = tn(f_here[...], all_rows(1, m)) * adapter_scale
            for h in range(HEADS):
                partial[m * HEADS + h] = rows[h * WIDTH : (h + 1) * WIDTH]
        take_over()

    for step in range(1, CHIPS):
        other = chip_at(step)
        landed(sum_land.at[other], sum_sems.at[1, other])
    total_all[core, chip] = jnp.sum(sum_land[...].astype(F32), axis=0).astype(BF16)
    for step in range(1, CHIPS):
        total_copy(chip_at(step)).start()
    pass_copy(chip).start()
    for step in range(1, CHIPS):
        other = chip_at(step)
        landed(total_all.at[core, other], total_sems.at[1, other])
        pass_copy(other).start()
    for origin in range(CHIPS):
        landed(total_all.at[1 - core, origin], twin_sems.at[1, origin])
    for block in range(BLOCKS):
        m, h = block // HEADS, block % HEADS
        columns = slice(h * WIDTH, (h + 1) * WIDTH)
        up_out[m, :, columns] = total_all[0, block // 2, block % 2].astype(F32)
        down_out[m, columns, :] = total_all[1, block // 2, block % 2].astype(F32)

    for kind in range(2):
        for phase in range(2):
            drain_heads(kind, phase)
    twin_copy.wait_send()
    for step in range(1, CHIPS):
        sum_copy(chip_at(step)).wait_send()
        total_copy(chip_at(step)).wait_send()
    for origin in range(CHIPS):
        pass_copy(origin).wait_send()

    def drain_sends(h, carry):
        for copy in query_copies(h) + key_copies(h):
            sent(*copy)
        return carry

    lax.fori_loop(0, HEADS, drain_sends, 0)

    @pl.when(working)
    def _drain_work():
        def one(origin, carry):
            for copy in pass_copies(origin) + (dq_pair_copy(origin),):
                move(*copy).wait_send()
            sent(*dq_copy(origin))
            sent(*dkv_copy(origin))
            return carry

        lax.fori_loop(0, CHIPS, one, 0)


def on_device(
    queries,
    key_matrix_rows,
    value_matrix_rows,
    attention_output,
    output_gradient,
    log_sum_norm,
    features,
    adapter_down_weight,
    adapter_up_weight,
    attended_key_blocks,
    used_block_count,
):
    vmem = pl.BlockSpec(memory_space=pltpu.VMEM)
    smem = pl.BlockSpec(memory_space=pltpu.SMEM)
    rows = jax.ShapeDtypeStruct((TOKENS, HEADS * WIDTH), BF16)
    down = jax.ShapeDtypeStruct((3, HEADS * WIDTH, WIDTH), F32)
    up = jax.ShapeDtypeStruct((3, WIDTH, HEADS * WIDTH), F32)
    dma = pltpu.SemaphoreType.DMA
    return pl.pallas_call(
        layer_kernel,
        out_shape=(rows, rows, rows, down, up),
        in_specs=[pl.BlockSpec(memory_space=pl.ANY)] * 9 + [smem] * 2,
        out_specs=(vmem,) * 5,
        scratch_shapes=[
            pltpu.VMEM((TOKENS, HEADS * WIDTH), BF16),
            pltpu.VMEM((TOKENS, HEADS * WIDTH), BF16),
            pltpu.VMEM((HEADS, TOKENS), F32),
            pltpu.VMEM((TOKENS, HEADS * WIDTH), BF16),
            pltpu.VMEM((3, HEADS * WIDTH, WIDTH), BF16),
            pltpu.VMEM((3, WIDTH, HEADS * WIDTH), BF16),
            dma((6,)),
            pltpu.VMEM((HEADS, 8, TOKENS), F32),
            pltpu.VMEM((CHIPS, 2, 8, TOKENS), F32),
            pltpu.VMEM((CHIPS, 2, 2, TOKENS, WIDTH), BF16),
            pltpu.VMEM((CHIPS, 2, TOKENS, WIDTH), BF16),
            pltpu.VMEM((WIDTH, TOKENS), BF16),
            pltpu.VMEM((TOKENS, WIDTH), F32),
            pltpu.VMEM((TOKENS, WIDTH), F32),
            pltpu.VMEM((CHIPS, 2, WIDTH, TOKENS), F32),
            pltpu.VMEM((CHIPS, WIDTH, TOKENS), F32),
            pltpu.VMEM((CHIPS, TOKENS, WIDTH), BF16),
            pltpu.VMEM((CHIPS, 2, TOKENS, WIDTH), BF16),
            pltpu.VMEM((HEADS, TOKENS, WIDTH), BF16),
            pltpu.VMEM((HEADS, 2, TOKENS, WIDTH), BF16),
            dma((HEADS,)), dma((2, HEADS)), dma((2, HEADS)), dma((2, CHIPS)),
            dma((CHIPS,)), dma((CHIPS,)), dma((CHIPS,)),
            dma((CHIPS,)), dma((CHIPS,)), dma((CHIPS,)), dma((2, CHIPS)),
            dma((CHIPS,)), dma((HEADS,)), dma((HEADS,)),
            pltpu.VMEM((2, GROUPS, 3, SHARE, WIDTH), BF16),
            pltpu.VMEM((2, GROUPS, 3, SHARE, WIDTH), BF16),
            pltpu.VMEM((2, GROUPS, 3, SHARE, WIDTH), BF16),
            dma((2, 2, 2, GROUPS)),
            pltpu.VMEM((BLOCKS, WIDTH, WIDTH), F32),
            pltpu.VMEM((BLOCKS, WIDTH, WIDTH), BF16),
            pltpu.VMEM((BLOCKS, WIDTH, WIDTH), BF16),
            pltpu.VMEM((CHIPS, 2, WIDTH, WIDTH), BF16),
            pltpu.VMEM((CHIPS, 2, WIDTH, WIDTH), BF16),
            pltpu.VMEM((2, CHIPS, 2, WIDTH, WIDTH), BF16),
            dma((2,)), dma((2, CHIPS)), dma((2, CHIPS)), dma((2, CHIPS)),
        ],
        compiler_params=pltpu.CompilerParams(
            collective_id=0, has_side_effects=True, vmem_limit_bytes=48 * 2**20
        ),
        name="layer",
    )(
        queries, key_matrix_rows, value_matrix_rows, attention_output, output_gradient,
        log_sum_norm, features, adapter_down_weight, adapter_up_weight,
        attended_key_blocks, used_block_count,
    )


def solution(mesh):
    placed = (
        P("ctx", "head"),
        P("ctx", "head"),
        P("ctx", "head"),
        P("ctx", "head"),
        P("ctx", "head"),
        P("head", "ctx"),
        P("ctx", "head"),
        P(None, "head", None),
        P(None, None, "head"),
        P("ctx", None),
        P("ctx"),
    )
    return jax.shard_map(
        on_device,
        mesh=mesh,
        in_specs=placed,
        out_specs=(
            P("ctx", "head"),
            P("ctx", "head"),
            P("ctx", "head"),
            P(None, "head", None),
            P(None, None, "head"),
        ),
        check_vma=False,
    )
```

```python
import functools
import math

import jax
import jax.numpy as jnp
from jax import lax
from jax.experimental import pallas as pl
from jax.experimental.pallas import tpu as pltpu
from jax.sharding import PartitionSpec as P

MESH = pl.DeviceIdType.MESH
BF16 = jnp.bfloat16
F32 = jnp.float32

HEADS = 5
WIDTH = 128
TOKENS = 256
RING = 16
BLOCK = 128
GROUPS = 8
SHARE = TOKENS // GROUPS
CHIPS = RING // 2
PIECE = HEADS * WIDTH // CHIPS
SCALE = WIDTH ** -0.5
LOG2E = math.log2(math.e)
DEAD = 1e30
adapter_scale = 0.125


def nt(a, b):
    return lax.dot_general(a, b, (((1,), (1,)), ((), ())), preferred_element_type=F32)


def nn(a, b):
    return lax.dot_general(a, b, (((1,), (0,)), ((), ())), preferred_element_type=F32)


def lane_slice(h):
    return pl.ds(pl.multiple_of(h * WIDTH, WIDTH), WIDTH)


def tn(a, b):
    return lax.dot_general(a, b, (((0,), (0,)), ((), ())), preferred_element_type=F32)


def layer_kernel(
    q_ref, k_ref, v_ref, o_ref, g_ref, lse_ref, f_ref, down_ref, up_ref, att_ref, used_ref,
    qg_ref, kg_ref, vg_ref, totals,
    o_here, g_here, lse_here, f_here, down_here, up_here, in_sems,
    stats, rs, rqg, rkv, keys_t, dk_acc, dv_acc, dq_acc, dq_land, dq_out, dkv_out, rdq, rdkv,
    s_send, qg_send, kv_send, pass_send, dq_pair_send, dq_send, dkv_send,
    s_recv, qg_recv, kv_recv, pass_recv, dq_pair_recv, dq_recv, dkv_recv,
    f_turned, projected_turned, row_send, row_land, row_all, row_sems,
    partial, pair_send, pair_land, sum_send, sum_land, pair_sems, sum_sems, total_sems, twin_sems,
):
    me = lax.axis_index("ctx")
    group = lax.axis_index("head")
    chip = me // 2
    core = lax.rem(me, 2)
    twin = me + 1 - 2 * core

    def chip_at(step):
        return lax.rem(chip + step, CHIPS)

    def move(src, dst, send_sem, recv_sem, target):
        return pltpu.make_async_remote_copy(
            src_ref=src, dst_ref=dst, send_sem=send_sem, recv_sem=recv_sem,
            device_id=(target, group), device_id_type=MESH,
        )

    def start(src, dst, send_sem, recv_sem, target):
        @pl.when(target != me)
        def _():
            move(src, dst, send_sem, recv_sem, target).start()

        @pl.when(target == me)
        def _():
            pltpu.make_async_copy(src, dst, recv_sem).start()

    def sent(src, dst, send_sem, recv_sem, target):
        @pl.when(target != me)
        def _():
            move(src, dst, send_sem, recv_sem, target).wait_send()

    def landed(dst, recv_sem):
        pltpu.make_async_copy(dst, dst, recv_sem).wait()

    barrier = pltpu.get_barrier_semaphore()

    def greet(step, carry):
        pl.semaphore_signal(
            barrier, inc=1, device_id=(2 * chip_at(step) + core, group), device_id_type=MESH
        )
        return carry

    def greet_head(step, carry):
        pl.semaphore_signal(
            barrier, inc=1, device_id=(me, lax.rem(group + step, GROUPS)), device_id_type=MESH
        )
        return carry

    pl.semaphore_signal(barrier, inc=1, device_id=(twin, group), device_id_type=MESH)
    lax.fori_loop(1, CHIPS, greet, 0)
    lax.fori_loop(1, GROUPS, greet_head, 0)

    inputs = [
        pltpu.make_async_copy(src, dst, in_sems.at[index])
        for index, (src, dst) in enumerate(
            (
                (g_ref, g_here), (o_ref, o_here), (lse_ref, lse_here),
                (f_ref, f_here), (down_ref, down_here), (up_ref, up_here),
            )
        )
    ]
    for copy in inputs:
        copy.start()

    lane = lax.broadcasted_iota(jnp.int32, (1, TOKENS), 1)
    words = [[jnp.int32(0), jnp.int32(0)], [jnp.int32(0), jnp.int32(0)]]
    for row in range(2):
        for slot in range(16):
            block = att_ref[row, slot]
            owner = jnp.right_shift(block, 1)
            bit = jnp.left_shift(jnp.int32(1), jnp.right_shift(block, 2) * 2 + (block & 1))
            for part in range(2):
                inside = ((owner & 1) == part) & (slot < used_ref[row])
                words[part][row] = words[part][row] | jnp.where(inside, bit, 0)
    codes = [
        jnp.where(lane < TOKENS // 2, word[0], word[1]).astype(F32) for word in words
    ]
    for copy in inputs[:3]:
        copy.wait()
    for h in range(HEADS):
        columns = slice(h * WIDTH, (h + 1) * WIDTH)
        product = g_here[:, columns].astype(F32) * o_here[:, columns].astype(F32)
        row_dot = jnp.sum(product.T, axis=0, keepdims=True)
        norm = lse_here[h : h + 1, :] * LOG2E
        stats[h] = jnp.concatenate(
            [norm, row_dot, codes[0], codes[1], jnp.zeros((4, TOKENS), F32)], axis=0
        )

    pl.semaphore_wait(barrier, CHIPS + GROUPS - 1)

    def query_copies(h):
        target = 2 * lax.rem(5 * h, CHIPS) + core
        lanes = lane_slice(h)
        return (
            (stats.at[h], rs.at[chip, core], s_send.at[h], s_recv.at[chip], target),
            (q_ref.at[:, lanes], rqg.at[chip, core, 0], qg_send.at[0, h], qg_recv.at[chip], target),
            (g_ref.at[:, lanes], rqg.at[chip, core, 1], qg_send.at[1, h], qg_recv.at[chip], target),
        )

    def key_copies(h):
        target = 2 * lax.rem(5 * h, CHIPS) + core
        lanes = lane_slice(h)
        return (
            (k_ref.at[:, lanes], rkv.at[chip, 0], kv_send.at[0, h], kv_recv.at[chip], target),
            (v_ref.at[:, lanes], rkv.at[chip, 1], kv_send.at[1, h], kv_recv.at[chip], target),
        )

    def send_all(copies):
        def one(step, carry):
            h = lax.rem(5 * lax.rem(chip - step + CHIPS, CHIPS), CHIPS)

            @pl.when(h < HEADS)
            def _():
                for copy in copies(h):
                    start(*copy)

            return carry

        lax.fori_loop(0, CHIPS, one, 0)

    send_all(query_copies)
    send_all(key_copies)

    def head_copy(kind, phase, m, other):
        if phase == 0:
            src, dst = row_send.at[kind, m, other], row_land.at[kind, m, group]
        else:
            src, dst = row_all.at[kind, m, group], row_all.at[kind, m, group]
        return pltpu.make_async_remote_copy(
            src_ref=src, dst_ref=dst,
            send_sem=row_sems.at[kind, phase, 0, m, other],
            recv_sem=row_sems.at[kind, phase, 1, m, group],
            device_id=(me, other), device_id_type=MESH,
        )

    def to_heads(kind, phase, m):
        def one(step, carry):
            head_copy(kind, phase, m, lax.rem(group + step, GROUPS)).start()
            return carry

        lax.fori_loop(1, GROUPS, one, 0)

    def from_heads(kind, phase, m):
        def one(step, carry):
            other = lax.rem(group + step, GROUPS)
            dst = (row_land if phase == 0 else row_all).at[kind, m, other]
            landed(dst, row_sems.at[kind, phase, 1, m, other])
            return carry

        lax.fori_loop(1, GROUPS, one, 0)

    def drain_heads(kind, phase, m):
        def one(step, carry):
            head_copy(kind, phase, m, lax.rem(group + step, GROUPS)).wait_send()
            return carry

        lax.fori_loop(1, GROUPS, one, 0)

    def split_rows(kind, m, rows):
        row_send[kind, m] = rows.astype(BF16).reshape(GROUPS, SHARE, WIDTH)
        to_heads(kind, 0, m)

    def sum_rows(kind, m):
        row_land[kind, m, group] = row_send[kind, m, group]
        from_heads(kind, 0, m)
        row_all[kind, m, group] = jnp.sum(row_land[kind, m].astype(F32), axis=0).astype(BF16)
        to_heads(kind, 1, m)

    def all_rows(kind, m):
        from_heads(kind, 1, m)
        return row_all[kind, m].reshape(TOKENS, WIDTH)

    inputs[3].wait()
    inputs[4].wait()
    for m in range(3):
        split_rows(0, m, nn(f_here[...], down_here[m]))
    f_turned[...] = f_here[...].astype(F32).T.astype(BF16)

    my_head = lax.rem(5 * chip, CHIPS)
    working = my_head < HEADS

    def pass_copies(origin):
        return (
            (rs.at[origin, core], rs.at[origin, core],
             pass_send.at[0, origin], pass_recv.at[0, origin], twin),
            (rqg.at[origin, core], rqg.at[origin, core],
             pass_send.at[1, origin], pass_recv.at[1, origin], twin),
        )

    def dq_pair_copy(origin):
        return (dq_acc.at[origin, 1 - core], dq_land.at[origin],
                dq_pair_send.at[origin], dq_pair_recv.at[origin], twin)

    def dq_copy(origin):
        return (dq_out.at[origin], rdq.at[my_head],
                dq_send.at[origin], dq_recv.at[my_head], 2 * origin + core)

    def dkv_copy(origin):
        return (dkv_out.at[origin], rdkv.at[my_head],
                dkv_send.at[origin], dkv_recv.at[my_head], 2 * origin + core)

    def compute(key_chip, origin, first):
        keys = rkv[key_chip, 0]
        queries = rqg[origin, :, 0].reshape(2 * TOKENS, WIDTH)
        grads = rqg[origin, :, 1].reshape(2 * TOKENS, WIDTH)
        norm = jnp.concatenate([rs[origin, side, 0:1, :] for side in range(2)], axis=1)
        row_dot = jnp.concatenate([rs[origin, side, 1:2, :] for side in range(2)], axis=1)
        code = jnp.concatenate(
            [
                jnp.where(core == 0, rs[origin, side, 2:3, :], rs[origin, side, 3:4, :])
                for side in range(2)
            ],
            axis=1,
        ).astype(jnp.int32)
        scores = nt(keys, queries)
        value_dot = nt(rkv[key_chip, 1], grads)
        low_parts, grad_parts = [], []
        for sub in range(2):
            bit = jnp.right_shift(code, key_chip * 2 + sub) & 1
            bias = jnp.where(bit > 0, norm, DEAD)
            piece = slice(sub * BLOCK, (sub + 1) * BLOCK)
            weights = jnp.exp2(scores[piece] * (SCALE * LOG2E) - bias)
            low_parts.append(weights.astype(BF16))
            grad_parts.append(
                (weights * ((value_dot[piece] - row_dot) * SCALE)).astype(BF16)
            )
        low = jnp.concatenate(low_parts, axis=0)
        score_grad = jnp.concatenate(grad_parts, axis=0)
        dv_acc[...] += nn(low, grads)
        dk_acc[...] += nn(score_grad, queries)
        dq_part = nn(keys_t[...], score_grad)
        for side in range(2):
            piece = dq_part[:, side * TOKENS : (side + 1) * TOKENS]
            if first:
                dq_acc[origin, side] = piece
            else:
                dq_acc[origin, side] += piece

    def open_keys(key_chip):
        landed(rkv.at[key_chip], kv_recv.at[key_chip])
        keys_t[...] = rkv[key_chip, 0].astype(F32).T.astype(BF16)
        dk_acc[...] = jnp.zeros_like(dk_acc)
        dv_acc[...] = jnp.zeros_like(dv_acc)

    def close_keys(key_chip):
        dkv_out[key_chip, 0] = dk_acc[...].astype(BF16)
        dkv_out[key_chip, 1] = dv_acc[...].astype(BF16)
        start(*dkv_copy(key_chip))

    @pl.when(working)
    def _first_keys():
        open_keys(chip)

        def receive(step, carry):
            origin = chip_at(step)
            landed(rs.at[origin, core], s_recv.at[origin])
            landed(rqg.at[origin, core], qg_recv.at[origin])
            for copy in pass_copies(origin):
                move(*copy).start()
            return carry

        def use(step, carry):
            origin = chip_at(step)
            landed(rs.at[origin, 1 - core], pass_recv.at[0, origin])
            landed(rqg.at[origin, 1 - core], pass_recv.at[1, origin])
            compute(chip, origin, True)
            return carry

        receive(0, 0)

        def both(step, carry):
            receive(step, carry)
            return use(step - 1, carry)

        lax.fori_loop(1, CHIPS, both, 0)
        use(CHIPS - 1, 0)
        close_keys(chip)

    for m in range(3):
        sum_rows(0, m)

    @pl.when(working)
    def _other_keys():
        def middle(turn, carry):
            key_chip = chip_at(turn)
            open_keys(key_chip)

            def one(step, inner):
                compute(key_chip, chip_at(step), False)
                return inner

            lax.fori_loop(0, CHIPS, one, 0, unroll=CHIPS)
            close_keys(key_chip)
            return carry

        lax.fori_loop(1, CHIPS - 1, middle, 0)

        key_chip = chip_at(CHIPS - 1)
        open_keys(key_chip)

        def finish(step):
            origin = chip_at(step)
            landed(dq_land.at[origin], dq_pair_recv.at[origin])
            total = dq_acc[origin, core] + dq_land[origin]
            dq_out[origin] = total.T.astype(BF16)
            start(*dq_copy(origin))

        def last(step, carry):
            origin = chip_at(step)
            compute(key_chip, origin, False)
            move(*dq_pair_copy(origin)).start()

            @pl.when(step > 0)
            def _():
                finish(step - 1)

            return carry

        lax.fori_loop(0, CHIPS, last, 0)
        close_keys(key_chip)
        finish(CHIPS - 1)

    for h in range(HEADS):
        columns = slice(h * WIDTH, (h + 1) * WIDTH)
        landed(rdkv.at[h], dkv_recv.at[h])
        kg_ref[:, columns] = rdkv[h, 0]
        vg_ref[:, columns] = rdkv[h, 1]
    for m in range(3):
        projected_turned[m] = all_rows(0, m).astype(F32).T.astype(BF16)
    inputs[5].wait()

    grads_out = (qg_ref, kg_ref, vg_ref)
    order = (1, 2, 0)

    def pair_copy(m):
        return move(pair_send.at[m], pair_land.at[m], pair_sems.at[0, m], pair_sems.at[1, m], twin)

    def sum_copy(m, other):
        return move(
            sum_send.at[m, other], sum_land.at[m, chip],
            sum_sems.at[0, m, other], sum_sems.at[1, m, chip], 2 * other + core,
        )

    def total_copy(m, other):
        return move(
            totals.at[core, m, chip], totals.at[core, m, chip],
            total_sems.at[0, m, other], total_sems.at[1, m, chip], 2 * other + core,
        )

    def twin_copy(m):
        return move(
            totals.at[core, m], totals.at[core, m], twin_sems.at[0, m], twin_sems.at[1, m], twin
        )

    def to_chips(copy, m):
        def one(step, carry):
            copy(m, chip_at(step)).start()
            return carry

        lax.fori_loop(1, CHIPS, one, 0)

    def from_chips(land, sems, m):
        def one(step, carry):
            other = chip_at(step)
            landed(land.at[m, other], sems.at[1, m, other])
            return carry

        lax.fori_loop(1, CHIPS, one, 0)

    def gather_rows(m):
        split_rows(1, m, nt(grads_out[m][...], up_here[m]))

    def up_rows(m):
        rows = nn(projected_turned[m], grads_out[m][...]) * adapter_scale
        for h in range(HEADS):
            partial[m, h * WIDTH : (h + 1) * WIDTH] = rows[:, h * WIDTH : (h + 1) * WIDTH]

        @pl.when(core == 1)
        def _():
            pair_send[m] = partial[m].astype(BF16)
            pair_copy(m).start()

    def down_rows(m):
        rows = nn(f_turned[...], all_rows(1, m)) * adapter_scale

        @pl.when(core == 0)
        def _():
            pair_send[m] = rows.astype(BF16)
            pair_copy(m).start()

        @pl.when(core == 1)
        def _():
            partial[m] = rows

    def sum_pair(m):
        pair_copy(m).wait_recv()
        both = partial[m] + pair_land[m].astype(F32)
        sum_send[m] = both.astype(BF16).reshape(CHIPS, PIECE, WIDTH)
        to_chips(sum_copy, m)
        sum_land[m, chip] = sum_send[m, chip]

    for m in order[:2]:
        gather_rows(m)
    for m in order[:2]:
        up_rows(m)
    for h in range(HEADS):
        landed(rdq.at[h], dq_recv.at[h])
        qg_ref[:, h * WIDTH : (h + 1) * WIDTH] = rdq[h]
    gather_rows(0)
    up_rows(0)
    for m in order:
        sum_rows(1, m)

    @pl.when(core == 0)
    def _up_sums():
        for m in order:
            sum_pair(m)

    for m in order:
        down_rows(m)

    @pl.when(core == 1)
    def _down_sums():
        for m in order:
            sum_pair(m)

    for m in order:
        from_chips(sum_land, sum_sems, m)
        totals[core, m, chip] = jnp.sum(sum_land[m].astype(F32), axis=0).astype(BF16)
        to_chips(total_copy, m)
    for m in order:
        from_chips(totals.at[core], total_sems, m)
        twin_copy(m).start()
    for m in order:
        landed(totals.at[1 - core, m], twin_sems.at[1, m])

    for m in range(3):
        for kind in range(2):
            for phase in range(2):
                drain_heads(kind, phase, m)
        pair_copy(m).wait_send()
        twin_copy(m).wait_send()

        def drain_chips(step, carry):
            sum_copy(m, chip_at(step)).wait_send()
            total_copy(m, chip_at(step)).wait_send()
            return carry

        lax.fori_loop(1, CHIPS, drain_chips, 0)

    def drain_sends(h, carry):
        for copy in query_copies(h) + key_copies(h):
            sent(*copy)
        return carry

    lax.fori_loop(0, HEADS, drain_sends, 0)

    @pl.when(working)
    def _drain_work():
        def one(origin, carry):
            for copy in pass_copies(origin) + (dq_pair_copy(origin),):
                move(*copy).wait_send()
            sent(*dq_copy(origin))
            sent(*dkv_copy(origin))
            return carry

        lax.fori_loop(0, CHIPS, one, 0)


def finish_kernel(q_in, k_in, v_in, totals, q_out, k_out, v_out, down_out, up_out):
    q_out[...] = q_in[...]
    k_out[...] = k_in[...]
    v_out[...] = v_in[...]
    down_out[...] = totals[1].astype(F32)
    for m in range(3):
        for h in range(HEADS):
            columns = slice(h * WIDTH, (h + 1) * WIDTH)
            up_out[m, :, columns] = totals[0, m, columns, :].astype(F32)


def finish(query_grad, key_grad, value_grad, totals):
    rows = jax.ShapeDtypeStruct(query_grad.shape, BF16)
    vmem = pl.BlockSpec(memory_space=pltpu.VMEM)
    return pl.pallas_call(
        finish_kernel,
        out_shape=(
            rows, rows, rows,
            jax.ShapeDtypeStruct((3, HEADS * WIDTH, WIDTH), F32),
            jax.ShapeDtypeStruct((3, WIDTH, HEADS * WIDTH), F32),
        ),
        in_specs=[vmem] * 4,
        out_specs=(vmem,) * 5,
        compiler_params=pltpu.CompilerParams(vmem_limit_bytes=60 * 2**20),
        name="finish",
    )(query_grad, key_grad, value_grad, totals.reshape(2, 3, HEADS * WIDTH, WIDTH))


def on_device(
    queries,
    key_matrix_rows,
    value_matrix_rows,
    attention_output,
    output_gradient,
    log_sum_norm,
    features,
    adapter_down_weight,
    adapter_up_weight,
    attended_key_blocks,
    used_block_count,
):
    vmem = pl.BlockSpec(memory_space=pltpu.VMEM)
    smem = pl.BlockSpec(memory_space=pltpu.SMEM)
    rows = jax.ShapeDtypeStruct((TOKENS, HEADS * WIDTH), BF16)
    totals = jax.ShapeDtypeStruct((2, 3, CHIPS, PIECE, WIDTH), BF16)
    dma = pltpu.SemaphoreType.DMA
    results = pl.pallas_call(
        layer_kernel,
        out_shape=(rows, rows, rows, totals),
        in_specs=[pl.BlockSpec(memory_space=pltpu.HBM)] * 9 + [smem] * 2,
        out_specs=(vmem,) * 4,
        scratch_shapes=[
            pltpu.VMEM((TOKENS, HEADS * WIDTH), BF16),
            pltpu.VMEM((TOKENS, HEADS * WIDTH), BF16),
            pltpu.VMEM((HEADS, TOKENS), F32),
            pltpu.VMEM((TOKENS, HEADS * WIDTH), BF16),
            pltpu.VMEM((3, HEADS * WIDTH, WIDTH), BF16),
            pltpu.VMEM((3, WIDTH, HEADS * WIDTH), BF16),
            dma((6,)),
            pltpu.VMEM((HEADS, 8, TOKENS), F32),
            pltpu.VMEM((CHIPS, 2, 8, TOKENS), F32),
            pltpu.VMEM((CHIPS, 2, 2, TOKENS, WIDTH), BF16),
            pltpu.VMEM((CHIPS, 2, TOKENS, WIDTH), BF16),
            pltpu.VMEM((WIDTH, TOKENS), BF16),
            pltpu.VMEM((TOKENS, WIDTH), F32),
            pltpu.VMEM((TOKENS, WIDTH), F32),
            pltpu.VMEM((CHIPS, 2, WIDTH, TOKENS), F32),
            pltpu.VMEM((CHIPS, WIDTH, TOKENS), F32),
            pltpu.VMEM((CHIPS, TOKENS, WIDTH), BF16),
            pltpu.VMEM((CHIPS, 2, TOKENS, WIDTH), BF16),
            pltpu.VMEM((HEADS, TOKENS, WIDTH), BF16),
            pltpu.VMEM((HEADS, 2, TOKENS, WIDTH), BF16),
            dma((HEADS,)), dma((2, HEADS)), dma((2, HEADS)), dma((2, CHIPS)),
            dma((CHIPS,)), dma((CHIPS,)), dma((CHIPS,)),
            dma((CHIPS,)), dma((CHIPS,)), dma((CHIPS,)), dma((2, CHIPS)),
            dma((CHIPS,)), dma((HEADS,)), dma((HEADS,)),
            pltpu.VMEM((HEADS * WIDTH, TOKENS), BF16),
            pltpu.VMEM((3, WIDTH, TOKENS), BF16),
            pltpu.VMEM((2, 3, GROUPS, SHARE, WIDTH), BF16),
            pltpu.VMEM((2, 3, GROUPS, SHARE, WIDTH), BF16),
            pltpu.VMEM((2, 3, GROUPS, SHARE, WIDTH), BF16),
            dma((2, 2, 2, 3, GROUPS)),
            pltpu.VMEM((3, HEADS * WIDTH, WIDTH), F32),
            pltpu.VMEM((3, HEADS * WIDTH, WIDTH), BF16),
            pltpu.VMEM((3, HEADS * WIDTH, WIDTH), BF16),
            pltpu.VMEM((3, CHIPS, PIECE, WIDTH), BF16),
            pltpu.VMEM((3, CHIPS, PIECE, WIDTH), BF16),
            dma((2, 3)), dma((2, 3, CHIPS)), dma((2, 3, CHIPS)), dma((2, 3)),
        ],
        compiler_params=pltpu.CompilerParams(
            collective_id=0, has_side_effects=True, vmem_limit_bytes=60 * 2**20
        ),
        name="layer",
    )(
        queries, key_matrix_rows, value_matrix_rows, attention_output, output_gradient,
        log_sum_norm, features, adapter_down_weight, adapter_up_weight,
        attended_key_blocks, used_block_count,
    )
    return finish(*results)


def solution(mesh):
    placed = (
        P("ctx", "head"),
        P("ctx", "head"),
        P("ctx", "head"),
        P("ctx", "head"),
        P("ctx", "head"),
        P("head", "ctx"),
        P("ctx", "head"),
        P(None, "head", None),
        P(None, None, "head"),
        P("ctx", None),
        P("ctx"),
    )
    return jax.shard_map(
        on_device,
        mesh=mesh,
        in_specs=placed,
        out_specs=(
            P("ctx", "head"),
            P("ctx", "head"),
            P("ctx", "head"),
            P(None, "head", None),
            P(None, None, "head"),
        ),
        check_vma=False,
    )
```

```python
import functools
import math

import jax
import jax.numpy as jnp
from jax import lax
from jax.experimental import pallas as pl
from jax.experimental.pallas import tpu as pltpu
from jax.sharding import PartitionSpec as P

MESH = pl.DeviceIdType.MESH
BF16 = jnp.bfloat16
F32 = jnp.float32

HEADS = 5
WIDTH = 128
TOKENS = 256
RING = 16
BLOCK = 128
EARLY = 4
LATE = 1
GROUPS = 8
SHARE = TOKENS // GROUPS
CHIPS = RING // 2
PIECE = HEADS * WIDTH // CHIPS
SCALE = WIDTH ** -0.5
LOG2E = math.log2(math.e)
DEAD = 1e30
adapter_scale = 0.125


def nt(a, b):
    return lax.dot_general(a, b, (((1,), (1,)), ((), ())), preferred_element_type=F32)


def nn(a, b):
    return lax.dot_general(a, b, (((1,), (0,)), ((), ())), preferred_element_type=F32)


def lane_slice(h):
    return pl.ds(pl.multiple_of(h * WIDTH, WIDTH), WIDTH)


def tn(a, b):
    return lax.dot_general(a, b, (((0,), (0,)), ((), ())), preferred_element_type=F32)


def layer_kernel(
    q_ref, k_ref, v_ref, o_ref, g_ref, lse_ref, f_ref, down_ref, up_ref, att_ref, used_ref,
    qg_ref, kg_ref, vg_ref, totals,
    o_here, g_here, lse_here, f_here, down_here, up_here, in_sems,
    stats, rs, rqg, rkv, keys_t, dk_acc, dv_acc, dq_acc, dq_land, dq_out, dkv_out, rdq, rdkv,
    s_send, qg_send, kv_send, pass_send, dq_pair_send, dq_send, dkv_send,
    s_recv, qg_recv, kv_recv, pass_recv, dq_pair_recv, dq_recv, dkv_recv,
    f_turned, f_twin, projected_turned, row_twin, row_twin_sems, f_twin_sems, row_send, row_land, row_all, row_sems,
    partial, pair_send, pair_land, sum_send, sum_land, pair_sems, sum_sems, total_sems, twin_sems,
):
    me = lax.axis_index("ctx")
    group = lax.axis_index("head")
    chip = me // 2
    core = lax.rem(me, 2)
    twin = me + 1 - 2 * core

    def chip_at(step):
        return lax.rem(chip + step, CHIPS)

    def move(src, dst, send_sem, recv_sem, target):
        return pltpu.make_async_remote_copy(
            src_ref=src, dst_ref=dst, send_sem=send_sem, recv_sem=recv_sem,
            device_id=(target, group), device_id_type=MESH,
        )

    def start(src, dst, send_sem, recv_sem, target):
        @pl.when(target != me)
        def _():
            move(src, dst, send_sem, recv_sem, target).start()

        @pl.when(target == me)
        def _():
            pltpu.make_async_copy(src, dst, recv_sem).start()

    def sent(src, dst, send_sem, recv_sem, target):
        @pl.when(target != me)
        def _():
            move(src, dst, send_sem, recv_sem, target).wait_send()

    def landed(dst, recv_sem):
        pltpu.make_async_copy(dst, dst, recv_sem).wait()

    barrier = pltpu.get_barrier_semaphore()

    def greet(step, carry):
        pl.semaphore_signal(
            barrier, inc=1, device_id=(2 * chip_at(step) + core, group), device_id_type=MESH
        )
        return carry

    def greet_head(step, carry):
        pl.semaphore_signal(
            barrier, inc=1, device_id=(me, lax.rem(group + step, GROUPS)), device_id_type=MESH
        )
        return carry

    pl.semaphore_signal(barrier, inc=1, device_id=(twin, group), device_id_type=MESH)
    lax.fori_loop(1, CHIPS, greet, 0)
    lax.fori_loop(1, GROUPS, greet_head, 0)

    inputs = [
        pltpu.make_async_copy(src, dst, in_sems.at[index])
        for index, (src, dst) in enumerate(
            (
                (g_ref, g_here), (o_ref, o_here), (lse_ref, lse_here),
                (f_ref, f_here), (down_ref, down_here), (up_ref, up_here),
            )
        )
    ]
    for copy in inputs:
        copy.start()

    pl.semaphore_wait(barrier, CHIPS + GROUPS - 1)

    def query_copies(h):
        target = 2 * lax.rem(5 * h, CHIPS) + core
        lanes = lane_slice(h)
        return (
            (q_ref.at[:, lanes], rqg.at[chip, core, 0], qg_send.at[0, h], qg_recv.at[chip], target),
            (g_ref.at[:, lanes], rqg.at[chip, core, 1], qg_send.at[1, h], qg_recv.at[chip], target),
        )

    def stats_copies(h):
        target = 2 * lax.rem(5 * h, CHIPS) + core
        return ((stats.at[h], rs.at[chip, core], s_send.at[h], s_recv.at[chip], target),)

    def key_copies(h):
        target = 2 * lax.rem(5 * h, CHIPS) + core
        lanes = lane_slice(h)
        return (
            (k_ref.at[:, lanes], rkv.at[chip, 0], kv_send.at[0, h], kv_recv.at[chip], target),
            (v_ref.at[:, lanes], rkv.at[chip, 1], kv_send.at[1, h], kv_recv.at[chip], target),
        )

    def send_some(copies, begin, end):
        def one(step, carry):
            h = lax.rem(5 * lax.rem(chip - step + CHIPS, CHIPS), CHIPS)

            @pl.when(h < HEADS)
            def _():
                for copy in copies(h):
                    start(*copy)

            return carry

        lax.fori_loop(begin, end, one, 0)

    send_some(key_copies, 0, EARLY)
    send_some(query_copies, 0, CHIPS)

    lane = lax.broadcasted_iota(jnp.int32, (1, TOKENS), 1)
    words = [[jnp.int32(0), jnp.int32(0)], [jnp.int32(0), jnp.int32(0)]]
    for row in range(2):
        for slot in range(16):
            block = att_ref[row, slot]
            owner = jnp.right_shift(block, 1)
            bit = jnp.left_shift(jnp.int32(1), jnp.right_shift(block, 2) * 2 + (block & 1))
            for part in range(2):
                inside = ((owner & 1) == part) & (slot < used_ref[row])
                words[part][row] = words[part][row] | jnp.where(inside, bit, 0)
    codes = [
        jnp.where(lane < TOKENS // 2, word[0], word[1]).astype(F32) for word in words
    ]
    for copy in inputs[:3]:
        copy.wait()
    for h in range(HEADS):
        columns = slice(h * WIDTH, (h + 1) * WIDTH)
        product = g_here[:, columns].astype(F32) * o_here[:, columns].astype(F32)
        row_dot = jnp.sum(product.T, axis=0, keepdims=True)
        norm = lse_here[h : h + 1, :] * LOG2E
        stats[h] = jnp.concatenate(
            [norm, row_dot, codes[0], codes[1], jnp.zeros((4, TOKENS), F32)], axis=0
        )

    send_some(stats_copies, 0, CHIPS)
    send_some(key_copies, EARLY, CHIPS)

    def head_copy(kind, phase, m, other):
        if phase == 0:
            src, dst = row_send.at[kind, m, other], row_land.at[kind, m, group]
        else:
            src, dst = row_all.at[kind, m, group], row_all.at[kind, m, group]
        return pltpu.make_async_remote_copy(
            src_ref=src, dst_ref=dst,
            send_sem=row_sems.at[kind, phase, 0, m, other],
            recv_sem=row_sems.at[kind, phase, 1, m, group],
            device_id=(me, other), device_id_type=MESH,
        )

    def to_heads(kind, phase, m):
        def one(step, carry):
            head_copy(kind, phase, m, lax.rem(group + step, GROUPS)).start()
            return carry

        lax.fori_loop(1, GROUPS, one, 0)

    def from_heads(kind, phase, m):
        def one(step, carry):
            other = lax.rem(group + step, GROUPS)
            dst = (row_land if phase == 0 else row_all).at[kind, m, other]
            landed(dst, row_sems.at[kind, phase, 1, m, other])
            return carry

        lax.fori_loop(1, GROUPS, one, 0)

    def drain_heads(kind, phase, m):
        def one(step, carry):
            head_copy(kind, phase, m, lax.rem(group + step, GROUPS)).wait_send()
            return carry

        lax.fori_loop(1, GROUPS, one, 0)

    def split_rows(kind, m, rows):
        row_send[kind, m] = rows.astype(BF16).reshape(GROUPS, SHARE, WIDTH)
        to_heads(kind, 0, m)

    def sum_rows(kind, m):
        row_land[kind, m, group] = row_send[kind, m, group]
        from_heads(kind, 0, m)
        row_all[kind, m, group] = jnp.sum(row_land[kind, m].astype(F32), axis=0).astype(BF16)
        to_heads(kind, 1, m)

    def all_rows(kind, m):
        from_heads(kind, 1, m)
        return row_all[kind, m].reshape(TOKENS, WIDTH)

    inputs[3].wait()
    inputs[4].wait()
    for m in range(3):
        split_rows(0, m, nn(f_here[...], down_here[m]))
    f_turned[...] = f_here[...].astype(F32).T.astype(BF16)
    f_copy = move(f_turned, f_twin, f_twin_sems.at[0], f_twin_sems.at[1], twin)

    @pl.when(core == 0)
    def _():
        f_copy.start()

    my_head = lax.rem(5 * chip, CHIPS)
    working = my_head < HEADS

    def pass_copies(origin):
        return (
            (rs.at[origin, core], rs.at[origin, core],
             pass_send.at[0, origin], pass_recv.at[0, origin], twin),
            (rqg.at[origin, core], rqg.at[origin, core],
             pass_send.at[1, origin], pass_recv.at[1, origin], twin),
        )

    def dq_pair_copy(origin):
        return (dq_acc.at[origin, 1 - core], dq_land.at[origin],
                dq_pair_send.at[origin], dq_pair_recv.at[origin], twin)

    def dq_copy(origin):
        return (dq_out.at[origin], rdq.at[my_head],
                dq_send.at[origin], dq_recv.at[my_head], 2 * origin + core)

    def dkv_copy(origin):
        return (dkv_out.at[origin], rdkv.at[my_head],
                dkv_send.at[origin], dkv_recv.at[my_head], 2 * origin + core)

    def compute(key_chip, slot, origin, first):
        keys = rkv[key_chip, 0]
        queries = rqg[origin, :, 0].reshape(2 * TOKENS, WIDTH)
        grads = rqg[origin, :, 1].reshape(2 * TOKENS, WIDTH)
        norm = jnp.concatenate([rs[origin, side, 0:1, :] for side in range(2)], axis=1)
        row_dot = jnp.concatenate([rs[origin, side, 1:2, :] for side in range(2)], axis=1)
        code = jnp.concatenate(
            [
                jnp.where(core == 0, rs[origin, side, 2:3, :], rs[origin, side, 3:4, :])
                for side in range(2)
            ],
            axis=1,
        ).astype(jnp.int32)
        scores = nt(keys, queries)
        value_dot = nt(rkv[key_chip, 1], grads)
        low_parts, grad_parts = [], []
        for sub in range(2):
            bit = jnp.right_shift(code, key_chip * 2 + sub) & 1
            bias = jnp.where(bit > 0, norm, DEAD)
            piece = slice(sub * BLOCK, (sub + 1) * BLOCK)
            weights = jnp.exp2(scores[piece] * (SCALE * LOG2E) - bias)
            low_parts.append(weights.astype(BF16))
            grad_parts.append(
                (weights * ((value_dot[piece] - row_dot) * SCALE)).astype(BF16)
            )
        low = jnp.concatenate(low_parts, axis=0)
        score_grad = jnp.concatenate(grad_parts, axis=0)
        dv_acc[slot] += nn(low, grads)
        dk_acc[slot] += nn(score_grad, queries)
        dq_part = nn(keys_t[slot], score_grad)
        for side in range(2):
            piece = dq_part[:, side * TOKENS : (side + 1) * TOKENS]
            if first:
                dq_acc[origin, side] = piece
            else:
                dq_acc[origin, side] += piece

    def open_keys(key_chip, slot):
        landed(rkv.at[key_chip], kv_recv.at[key_chip])
        keys_t[slot] = rkv[key_chip, 0].astype(F32).T.astype(BF16)
        dk_acc[slot] = jnp.zeros((TOKENS, WIDTH), F32)
        dv_acc[slot] = jnp.zeros((TOKENS, WIDTH), F32)

    def close_keys(key_chip, slot):
        dkv_out[key_chip, 0] = dk_acc[slot].astype(BF16)
        dkv_out[key_chip, 1] = dv_acc[slot].astype(BF16)
        start(*dkv_copy(key_chip))

    @pl.when(working)
    def _first_keys():
        def receive(step):
            origin = chip_at(step)
            landed(rs.at[origin, core], s_recv.at[origin])
            landed(rqg.at[origin, core], qg_recv.at[origin])
            for copy in pass_copies(origin):
                move(*copy).start()

        def use(step):
            origin = chip_at(step)
            landed(rs.at[origin, 1 - core], pass_recv.at[0, origin])
            landed(rqg.at[origin, 1 - core], pass_recv.at[1, origin])
            for slot in range(EARLY):
                compute(chip_at(slot), slot, origin, slot == 0)

        for slot in range(EARLY):
            open_keys(chip_at(slot), slot)
        receive(0)

        def both(step, carry):
            receive(step)
            use(step - 1)
            return carry

        lax.fori_loop(1, CHIPS, both, 0)
        use(CHIPS - 1)
        for slot in range(EARLY):
            close_keys(chip_at(slot), slot)

    for m in range(3):
        sum_rows(0, m)

    @pl.when(working)
    def _other_keys():
        def middle(turn, carry):
            key_chip = chip_at(turn)
            open_keys(key_chip, 0)

            def one(step, inner):
                compute(key_chip, 0, chip_at(step), False)
                return inner

            lax.fori_loop(0, CHIPS, one, 0, unroll=CHIPS)
            close_keys(key_chip, 0)
            return carry

        lax.fori_loop(EARLY, CHIPS - LATE, middle, 0)

        late = [chip_at(CHIPS - LATE + slot) for slot in range(LATE)]
        for slot in range(LATE):
            open_keys(late[slot], slot)

        def finish_query(step):
            origin = chip_at(step)
            landed(dq_land.at[origin], dq_pair_recv.at[origin])
            total = dq_acc[origin, core] + dq_land[origin]
            dq_out[origin] = total.T.astype(BF16)
            start(*dq_copy(origin))

        for step in range(0, CHIPS, 2):
            for place in (step, step + 1):
                for slot in range(LATE):
                    compute(late[slot], slot, chip_at(place), False)
            for place in (step, step + 1):
                move(*dq_pair_copy(chip_at(place))).start()
            if step > 0:
                finish_query(step - 2)
                finish_query(step - 1)
        for slot in range(LATE):
            close_keys(late[slot], slot)
        finish_query(CHIPS - 2)
        finish_query(CHIPS - 1)

    for h in range(HEADS):
        columns = slice(h * WIDTH, (h + 1) * WIDTH)
        landed(rdkv.at[h], dkv_recv.at[h])
        kg_ref[:, columns] = rdkv[h, 0]
        vg_ref[:, columns] = rdkv[h, 1]
    inputs[5].wait()
    for m in range(3):
        projected_turned[m] = all_rows(0, m).astype(F32).T.astype(BF16)

    grads_out = (qg_ref, kg_ref, vg_ref)
    order = (1, 2, 0)

    def pair_copy(m):
        return move(pair_send.at[m], pair_land.at[m], pair_sems.at[0, m], pair_sems.at[1, m], twin)

    def sum_copy(m, other):
        return move(
            sum_send.at[m, other], sum_land.at[m, chip],
            sum_sems.at[0, m, other], sum_sems.at[1, m, chip], 2 * other + core,
        )

    def total_copy(m, other):
        return move(
            totals.at[core, m, chip], totals.at[core, m, chip],
            total_sems.at[0, m, other], total_sems.at[1, m, chip], 2 * other + core,
        )

    def twin_copy(m):
        return move(
            totals.at[core, m], totals.at[core, m], twin_sems.at[0, m], twin_sems.at[1, m], twin
        )

    def to_chips(copy, m):
        def one(step, carry):
            copy(m, chip_at(step)).start()
            return carry

        lax.fori_loop(1, CHIPS, one, 0)

    def from_chips(land, sems, m):
        def one(step, carry):
            other = chip_at(step)
            landed(land.at[m, other], sems.at[1, m, other])
            return carry

        lax.fori_loop(1, CHIPS, one, 0)

    def gather_rows(m):
        split_rows(1, m, nt(grads_out[m][...], up_here[m]))

    def up_rows(m):
        rows = nn(projected_turned[m], grads_out[m][...]) * adapter_scale
        for h in range(HEADS):
            partial[m, h * WIDTH : (h + 1) * WIDTH] = rows[:, h * WIDTH : (h + 1) * WIDTH]

        @pl.when(core == 1)
        def _():
            pair_send[m] = partial[m].astype(BF16)
            pair_copy(m).start()

    def row_copy(m):
        return move(
            row_all.at[1, m], row_twin.at[m], row_twin_sems.at[0, m], row_twin_sems.at[1, m], twin
        )

    def to_sums(m, rows):
        sum_send[m] = rows.astype(BF16).reshape(CHIPS, PIECE, WIDTH)
        to_chips(sum_copy, m)
        sum_land[m, chip] = sum_send[m, chip]

    def up_sum(m):
        pair_copy(m).wait_recv()
        to_sums(m, partial[m] + pair_land[m].astype(F32))

    def down_sum(m):
        rows = nn(f_turned[...], all_rows(1, m))
        row_copy(m).wait_recv()
        rows += nn(f_twin[...], row_twin[m].reshape(TOKENS, WIDTH))
        to_sums(m, rows * adapter_scale)

    for m in order[:2]:
        gather_rows(m)
    for h in range(HEADS):
        landed(rdq.at[h], dq_recv.at[h])
        qg_ref[:, h * WIDTH : (h + 1) * WIDTH] = rdq[h]
    gather_rows(0)
    for m in order:
        up_rows(m)
    for m in order:
        sum_rows(1, m)

    @pl.when(core == 0)
    def _up_sums():
        for m in order:
            up_sum(m)
        for m in order:
            from_heads(1, 1, m)
            row_copy(m).start()

    @pl.when(core == 1)
    def _down_sums():
        f_copy.wait_recv()
        for m in order:
            down_sum(m)

    for m in order:
        from_chips(sum_land, sum_sems, m)
        totals[core, m, chip] = jnp.sum(sum_land[m].astype(F32), axis=0).astype(BF16)
        to_chips(total_copy, m)
    for m in order:
        from_chips(totals.at[core], total_sems, m)
        twin_copy(m).start()
    for m in order:
        landed(totals.at[1 - core, m], twin_sems.at[1, m])

    for m in range(3):
        for kind in range(2):
            for phase in range(2):
                drain_heads(kind, phase, m)
        twin_copy(m).wait_send()

        def drain_chips(step, carry):
            sum_copy(m, chip_at(step)).wait_send()
            total_copy(m, chip_at(step)).wait_send()
            return carry

        lax.fori_loop(1, CHIPS, drain_chips, 0)

    @pl.when(core == 0)
    def _drain_rows():
        f_copy.wait_send()
        for m in range(3):
            row_copy(m).wait_send()

    @pl.when(core == 1)
    def _drain_pairs():
        for m in range(3):
            pair_copy(m).wait_send()

    def drain_sends(h, carry):
        for copy in query_copies(h) + stats_copies(h) + key_copies(h):
            sent(*copy)
        return carry

    lax.fori_loop(0, HEADS, drain_sends, 0)

    @pl.when(working)
    def _drain_work():
        def one(origin, carry):
            for copy in pass_copies(origin) + (dq_pair_copy(origin),):
                move(*copy).wait_send()
            sent(*dq_copy(origin))
            sent(*dkv_copy(origin))
            return carry

        lax.fori_loop(0, CHIPS, one, 0)


def finish_kernel(q_in, k_in, v_in, totals, q_out, k_out, v_out, down_out, up_out):
    q_out[...] = q_in[...]
    k_out[...] = k_in[...]
    v_out[...] = v_in[...]
    down_out[...] = totals[1].astype(F32)
    for m in range(3):
        for h in range(HEADS):
            columns = slice(h * WIDTH, (h + 1) * WIDTH)
            up_out[m, :, columns] = totals[0, m, columns, :].astype(F32)


def finish(query_grad, key_grad, value_grad, totals):
    rows = jax.ShapeDtypeStruct(query_grad.shape, BF16)
    vmem = pl.BlockSpec(memory_space=pltpu.VMEM)
    return pl.pallas_call(
        finish_kernel,
        out_shape=(
            rows, rows, rows,
            jax.ShapeDtypeStruct((3, HEADS * WIDTH, WIDTH), F32),
            jax.ShapeDtypeStruct((3, WIDTH, HEADS * WIDTH), F32),
        ),
        in_specs=[vmem] * 4,
        out_specs=(vmem,) * 5,
        compiler_params=pltpu.CompilerParams(vmem_limit_bytes=60 * 2**20),
        name="finish",
    )(query_grad, key_grad, value_grad, totals.reshape(2, 3, HEADS * WIDTH, WIDTH))


def on_device(
    queries,
    key_matrix_rows,
    value_matrix_rows,
    attention_output,
    output_gradient,
    log_sum_norm,
    features,
    adapter_down_weight,
    adapter_up_weight,
    attended_key_blocks,
    used_block_count,
):
    vmem = pl.BlockSpec(memory_space=pltpu.VMEM)
    smem = pl.BlockSpec(memory_space=pltpu.SMEM)
    rows = jax.ShapeDtypeStruct((TOKENS, HEADS * WIDTH), BF16)
    totals = jax.ShapeDtypeStruct((2, 3, CHIPS, PIECE, WIDTH), BF16)
    dma = pltpu.SemaphoreType.DMA
    results = pl.pallas_call(
        layer_kernel,
        out_shape=(rows, rows, rows, totals),
        in_specs=[pl.BlockSpec(memory_space=pltpu.HBM)] * 9 + [smem] * 2,
        out_specs=(vmem,) * 4,
        scratch_shapes=[
            pltpu.VMEM((TOKENS, HEADS * WIDTH), BF16),
            pltpu.VMEM((TOKENS, HEADS * WIDTH), BF16),
            pltpu.VMEM((HEADS, TOKENS), F32),
            pltpu.VMEM((TOKENS, HEADS * WIDTH), BF16),
            pltpu.VMEM((3, HEADS * WIDTH, WIDTH), BF16),
            pltpu.VMEM((3, WIDTH, HEADS * WIDTH), BF16),
            dma((6,)),
            pltpu.VMEM((HEADS, 8, TOKENS), F32),
            pltpu.VMEM((CHIPS, 2, 8, TOKENS), F32),
            pltpu.VMEM((CHIPS, 2, 2, TOKENS, WIDTH), BF16),
            pltpu.VMEM((CHIPS, 2, TOKENS, WIDTH), BF16),
            pltpu.VMEM((EARLY, WIDTH, TOKENS), BF16),
            pltpu.VMEM((EARLY, TOKENS, WIDTH), F32),
            pltpu.VMEM((EARLY, TOKENS, WIDTH), F32),
            pltpu.VMEM((CHIPS, 2, WIDTH, TOKENS), F32),
            pltpu.VMEM((CHIPS, WIDTH, TOKENS), F32),
            pltpu.VMEM((CHIPS, TOKENS, WIDTH), BF16),
            pltpu.VMEM((CHIPS, 2, TOKENS, WIDTH), BF16),
            pltpu.VMEM((HEADS, TOKENS, WIDTH), BF16),
            pltpu.VMEM((HEADS, 2, TOKENS, WIDTH), BF16),
            dma((HEADS,)), dma((2, HEADS)), dma((2, HEADS)), dma((2, CHIPS)),
            dma((CHIPS,)), dma((CHIPS,)), dma((CHIPS,)),
            dma((CHIPS,)), dma((CHIPS,)), dma((CHIPS,)), dma((2, CHIPS)),
            dma((CHIPS,)), dma((HEADS,)), dma((HEADS,)),
            pltpu.VMEM((HEADS * WIDTH, TOKENS), BF16),
            pltpu.VMEM((HEADS * WIDTH, TOKENS), BF16),
            pltpu.VMEM((3, WIDTH, TOKENS), BF16),
            pltpu.VMEM((3, GROUPS, SHARE, WIDTH), BF16),
            dma((2, 3)), dma((2,)),
            pltpu.VMEM((2, 3, GROUPS, SHARE, WIDTH), BF16),
            pltpu.VMEM((2, 3, GROUPS, SHARE, WIDTH), BF16),
            pltpu.VMEM((2, 3, GROUPS, SHARE, WIDTH), BF16),
            dma((2, 2, 2, 3, GROUPS)),
            pltpu.VMEM((3, HEADS * WIDTH, WIDTH), F32),
            pltpu.VMEM((3, HEADS * WIDTH, WIDTH), BF16),
            pltpu.VMEM((3, HEADS * WIDTH, WIDTH), BF16),
            pltpu.VMEM((3, CHIPS, PIECE, WIDTH), BF16),
            pltpu.VMEM((3, CHIPS, PIECE, WIDTH), BF16),
            dma((2, 3)), dma((2, 3, CHIPS)), dma((2, 3, CHIPS)), dma((2, 3)),
        ],
        compiler_params=pltpu.CompilerParams(
            collective_id=0, has_side_effects=True, vmem_limit_bytes=60 * 2**20
        ),
        name="layer",
    )(
        queries, key_matrix_rows, value_matrix_rows, attention_output, output_gradient,
        log_sum_norm, features, adapter_down_weight, adapter_up_weight,
        attended_key_blocks, used_block_count,
    )
    return finish(*results)


def solution(mesh):
    placed = (
        P("ctx", "head"),
        P("ctx", "head"),
        P("ctx", "head"),
        P("ctx", "head"),
        P("ctx", "head"),
        P("head", "ctx"),
        P("ctx", "head"),
        P(None, "head", None),
        P(None, None, "head"),
        P("ctx", None),
        P("ctx"),
    )
    return jax.shard_map(
        on_device,
        mesh=mesh,
        in_specs=placed,
        out_specs=(
            P("ctx", "head"),
            P("ctx", "head"),
            P("ctx", "head"),
            P(None, "head", None),
            P(None, None, "head"),
        ),
        check_vma=False,
    )
```

```python
import functools
import math

import jax
import jax.numpy as jnp
from jax import lax
from jax.experimental import pallas as pl
from jax.experimental.pallas import tpu as pltpu
from jax.sharding import PartitionSpec as P

MESH = pl.DeviceIdType.MESH
BF16 = jnp.bfloat16
F32 = jnp.float32

HEADS = 5
WIDTH = 128
TOKENS = 256
RING = 16
BLOCK = 128
EARLY = 4
LATE = 1
GROUPS = 8
SHARE = TOKENS // GROUPS
CHIPS = RING // 2
PIECE = HEADS * WIDTH // CHIPS
SCALE = WIDTH ** -0.5
LOG2E = math.log2(math.e)
DEAD = 1e30
adapter_scale = 0.125


def nt(a, b):
    return lax.dot_general(a, b, (((1,), (1,)), ((), ())), preferred_element_type=F32)


def nn(a, b):
    return lax.dot_general(a, b, (((1,), (0,)), ((), ())), preferred_element_type=F32)


def lane_slice(h):
    return pl.ds(pl.multiple_of(h * WIDTH, WIDTH), WIDTH)


def tn(a, b):
    return lax.dot_general(a, b, (((0,), (0,)), ((), ())), preferred_element_type=F32)


def layer_kernel(
    q_ref, k_ref, v_ref, o_ref, g_ref, lse_ref, f_ref, down_ref, up_ref, att_ref, used_ref,
    q_out, k_out, v_out, totals,
    qg_ref, kg_ref, vg_ref, out_sems,
    o_here, g_here, lse_here, f_here, down_here, up_here, in_sems,
    stats, rs, rqg, rkv, keys_t, dk_acc, dv_acc, dq_acc, dq_land, dq_out, dkv_out, rdq, rdkv,
    s_send, qg_send, kv_send, pass_send, dq_pair_send, dq_send, dkv_send,
    s_recv, qg_recv, kv_recv, pass_recv, dq_pair_recv, dq_recv, dkv_recv,
    f_turned, f_twin, projected_turned, row_twin, row_twin_sems, f_twin_sems, row_send, row_land, row_all, row_sems,
    partial, pair_send, pair_land, sum_send, sum_land, pair_sems, sum_sems, total_sems, twin_sems,
):
    me = lax.axis_index("ctx")
    group = lax.axis_index("head")
    chip = me // 2
    core = lax.rem(me, 2)
    twin = me + 1 - 2 * core

    def chip_at(step):
        return lax.rem(chip + step, CHIPS)

    def move(src, dst, send_sem, recv_sem, target):
        return pltpu.make_async_remote_copy(
            src_ref=src, dst_ref=dst, send_sem=send_sem, recv_sem=recv_sem,
            device_id=(target, group), device_id_type=MESH,
        )

    def start(src, dst, send_sem, recv_sem, target):
        @pl.when(target != me)
        def _():
            move(src, dst, send_sem, recv_sem, target).start()

        @pl.when(target == me)
        def _():
            pltpu.make_async_copy(src, dst, recv_sem).start()

    def sent(src, dst, send_sem, recv_sem, target):
        @pl.when(target != me)
        def _():
            move(src, dst, send_sem, recv_sem, target).wait_send()

    def landed(dst, recv_sem):
        pltpu.make_async_copy(dst, dst, recv_sem).wait()

    barrier = pltpu.get_barrier_semaphore()

    def greet(step, carry):
        pl.semaphore_signal(
            barrier, inc=1, device_id=(2 * chip_at(step) + core, group), device_id_type=MESH
        )
        return carry

    def greet_head(step, carry):
        pl.semaphore_signal(
            barrier, inc=1, device_id=(me, lax.rem(group + step, GROUPS)), device_id_type=MESH
        )
        return carry

    pl.semaphore_signal(barrier, inc=1, device_id=(twin, group), device_id_type=MESH)
    lax.fori_loop(1, CHIPS, greet, 0)
    lax.fori_loop(1, GROUPS, greet_head, 0)

    inputs = [
        pltpu.make_async_copy(src, dst, in_sems.at[index])
        for index, (src, dst) in enumerate(
            (
                (g_ref, g_here), (o_ref, o_here), (lse_ref, lse_here),
                (f_ref, f_here), (down_ref, down_here), (up_ref, up_here),
            )
        )
    ]
    for copy in inputs:
        copy.start()

    pl.semaphore_wait(barrier, CHIPS + GROUPS - 1)

    def query_copies(h):
        target = 2 * lax.rem(5 * h, CHIPS) + core
        lanes = lane_slice(h)
        return (
            (q_ref.at[:, lanes], rqg.at[chip, core, 0], qg_send.at[0, h], qg_recv.at[chip], target),
            (g_ref.at[:, lanes], rqg.at[chip, core, 1], qg_send.at[1, h], qg_recv.at[chip], target),
        )

    def stats_copies(h):
        target = 2 * lax.rem(5 * h, CHIPS) + core
        return ((stats.at[h], rs.at[chip, core], s_send.at[h], s_recv.at[chip], target),)

    def key_copies(h):
        target = 2 * lax.rem(5 * h, CHIPS) + core
        lanes = lane_slice(h)
        return (
            (k_ref.at[:, lanes], rkv.at[chip, 0], kv_send.at[0, h], kv_recv.at[chip], target),
            (v_ref.at[:, lanes], rkv.at[chip, 1], kv_send.at[1, h], kv_recv.at[chip], target),
        )

    def send_some(copies, begin, end):
        def one(step, carry):
            h = lax.rem(5 * lax.rem(chip - step + CHIPS, CHIPS), CHIPS)

            @pl.when(h < HEADS)
            def _():
                for copy in copies(h):
                    start(*copy)

            return carry

        lax.fori_loop(begin, end, one, 0)

    send_some(key_copies, 0, EARLY)
    send_some(query_copies, 0, CHIPS)

    lane = lax.broadcasted_iota(jnp.int32, (1, TOKENS), 1)
    words = [[jnp.int32(0), jnp.int32(0)], [jnp.int32(0), jnp.int32(0)]]
    for row in range(2):
        for slot in range(16):
            block = att_ref[row, slot]
            owner = jnp.right_shift(block, 1)
            bit = jnp.left_shift(jnp.int32(1), jnp.right_shift(block, 2) * 2 + (block & 1))
            for part in range(2):
                inside = ((owner & 1) == part) & (slot < used_ref[row])
                words[part][row] = words[part][row] | jnp.where(inside, bit, 0)
    codes = [
        jnp.where(lane < TOKENS // 2, word[0], word[1]).astype(F32) for word in words
    ]
    for copy in inputs[:3]:
        copy.wait()
    for h in range(HEADS):
        columns = slice(h * WIDTH, (h + 1) * WIDTH)
        product = g_here[:, columns].astype(F32) * o_here[:, columns].astype(F32)
        row_dot = jnp.sum(product.T, axis=0, keepdims=True)
        norm = lse_here[h : h + 1, :] * LOG2E
        stats[h] = jnp.concatenate(
            [norm, row_dot, codes[0], codes[1]], axis=0
        )

    send_some(stats_copies, 0, CHIPS)
    send_some(key_copies, EARLY, CHIPS)

    def head_copy(kind, phase, m, other):
        if phase == 0:
            src, dst = row_send.at[kind, m, other], row_land.at[kind, m, group]
        else:
            src, dst = row_all.at[kind, m, group], row_all.at[kind, m, group]
        return pltpu.make_async_remote_copy(
            src_ref=src, dst_ref=dst,
            send_sem=row_sems.at[kind, phase, 0, m, other],
            recv_sem=row_sems.at[kind, phase, 1, m, group],
            device_id=(me, other), device_id_type=MESH,
        )

    def to_heads(kind, phase, m):
        def one(step, carry):
            head_copy(kind, phase, m, lax.rem(group + step, GROUPS)).start()
            return carry

        lax.fori_loop(1, GROUPS, one, 0)

    def from_heads(kind, phase, m):
        def one(step, carry):
            other = lax.rem(group + step, GROUPS)
            dst = (row_land if phase == 0 else row_all).at[kind, m, other]
            landed(dst, row_sems.at[kind, phase, 1, m, other])
            return carry

        lax.fori_loop(1, GROUPS, one, 0)

    def drain_heads(kind, phase, m):
        def one(step, carry):
            head_copy(kind, phase, m, lax.rem(group + step, GROUPS)).wait_send()
            return carry

        lax.fori_loop(1, GROUPS, one, 0)

    def split_rows(kind, m, rows):
        row_send[kind, m] = rows.astype(BF16).reshape(GROUPS, SHARE, WIDTH)
        to_heads(kind, 0, m)

    def sum_rows(kind, m):
        row_land[kind, m, group] = row_send[kind, m, group]
        from_heads(kind, 0, m)
        row_all[kind, m, group] = jnp.sum(row_land[kind, m].astype(F32), axis=0).astype(BF16)
        to_heads(kind, 1, m)

    def all_rows(kind, m):
        from_heads(kind, 1, m)
        return row_all[kind, m].reshape(TOKENS, WIDTH)

    inputs[3].wait()
    inputs[4].wait()
    for m in range(3):
        split_rows(0, m, nn(f_here[...], down_here[m]))
    f_turned[...] = f_here[...].astype(F32).T.astype(BF16)
    f_copy = move(f_turned, f_twin, f_twin_sems.at[0], f_twin_sems.at[1], twin)

    @pl.when(core == 0)
    def _():
        f_copy.start()

    my_head = lax.rem(5 * chip, CHIPS)
    working = my_head < HEADS

    def pass_copies(origin):
        return (
            (rs.at[origin, core], rs.at[origin, core],
             pass_send.at[0, origin], pass_recv.at[0, origin], twin),
            (rqg.at[origin, core], rqg.at[origin, core],
             pass_send.at[1, origin], pass_recv.at[1, origin], twin),
        )

    def dq_pair_copy(origin):
        return (dq_acc.at[origin, 1 - core], dq_land.at[origin],
                dq_pair_send.at[origin], dq_pair_recv.at[origin], twin)

    def dq_copy(origin):
        return (dq_out.at[origin], rdq.at[my_head],
                dq_send.at[origin], dq_recv.at[my_head], 2 * origin + core)

    def dkv_copy(origin):
        return (dkv_out.at[origin], rdkv.at[my_head],
                dkv_send.at[origin], dkv_recv.at[my_head], 2 * origin + core)

    def compute(key_chip, slot, origin, first):
        keys = rkv[key_chip, 0]
        queries = rqg[origin, :, 0].reshape(2 * TOKENS, WIDTH)
        grads = rqg[origin, :, 1].reshape(2 * TOKENS, WIDTH)
        norm = jnp.concatenate([rs[origin, side, 0:1, :] for side in range(2)], axis=1)
        row_dot = jnp.concatenate([rs[origin, side, 1:2, :] for side in range(2)], axis=1)
        code = jnp.concatenate(
            [
                jnp.where(core == 0, rs[origin, side, 2:3, :], rs[origin, side, 3:4, :])
                for side in range(2)
            ],
            axis=1,
        ).astype(jnp.int32)
        scores = nt(keys, queries)
        value_dot = nt(rkv[key_chip, 1], grads)
        low_parts, grad_parts = [], []
        for sub in range(2):
            bit = jnp.right_shift(code, key_chip * 2 + sub) & 1
            bias = jnp.where(bit > 0, norm, DEAD)
            piece = slice(sub * BLOCK, (sub + 1) * BLOCK)
            weights = jnp.exp2(scores[piece] * (SCALE * LOG2E) - bias)
            low_parts.append(weights.astype(BF16))
            grad_parts.append(
                (weights * ((value_dot[piece] - row_dot) * SCALE)).astype(BF16)
            )
        low = jnp.concatenate(low_parts, axis=0)
        score_grad = jnp.concatenate(grad_parts, axis=0)
        dv_acc[slot] += nn(low, grads)
        dk_acc[slot] += nn(score_grad, queries)
        dq_part = nn(keys_t[slot], score_grad)
        for side in range(2):
            piece = dq_part[:, side * TOKENS : (side + 1) * TOKENS]
            if first:
                dq_acc[origin, side] = piece
            else:
                dq_acc[origin, side] += piece

    def open_keys(key_chip, slot):
        landed(rkv.at[key_chip], kv_recv.at[key_chip])
        keys_t[slot] = rkv[key_chip, 0].astype(F32).T.astype(BF16)
        dk_acc[slot] = jnp.zeros((TOKENS, WIDTH), F32)
        dv_acc[slot] = jnp.zeros((TOKENS, WIDTH), F32)

    def close_keys(key_chip, slot):
        dkv_out[key_chip, 0] = dk_acc[slot].astype(BF16)
        dkv_out[key_chip, 1] = dv_acc[slot].astype(BF16)
        start(*dkv_copy(key_chip))

    @pl.when(working)
    def _first_keys():
        def receive(step):
            origin = chip_at(step)
            landed(rs.at[origin, core], s_recv.at[origin])
            landed(rqg.at[origin, core], qg_recv.at[origin])
            for copy in pass_copies(origin):
                move(*copy).start()

        def use(step):
            origin = chip_at(step)
            landed(rs.at[origin, 1 - core], pass_recv.at[0, origin])
            landed(rqg.at[origin, 1 - core], pass_recv.at[1, origin])
            for slot in range(EARLY):
                compute(chip_at(slot), slot, origin, slot == 0)

        for slot in range(EARLY):
            open_keys(chip_at(slot), slot)
        receive(0)

        def both(step, carry):
            @pl.when(step < CHIPS)
            def _():
                receive(step)

            @pl.when(step == 5)
            def _():
                for m in range(3):
                    sum_rows(0, m)

            use(step - 1)
            return carry

        lax.fori_loop(1, CHIPS + 1, both, 0)
        for slot in range(EARLY):
            close_keys(chip_at(slot), slot)

    @pl.when(my_head >= HEADS)
    def _idle():
        for m in range(3):
            sum_rows(0, m)

    @pl.when(working)
    def _other_keys():
        def middle(turn, carry):
            key_chip = chip_at(turn)
            open_keys(key_chip, 0)

            def one(step, inner):
                compute(key_chip, 0, chip_at(step), False)
                return inner

            lax.fori_loop(0, CHIPS, one, 0, unroll=CHIPS)
            close_keys(key_chip, 0)
            return carry

        lax.fori_loop(EARLY, CHIPS - LATE, middle, 0)

        late = [chip_at(CHIPS - LATE + slot) for slot in range(LATE)]
        for slot in range(LATE):
            open_keys(late[slot], slot)

        def finish_query(step):
            origin = chip_at(step)
            landed(dq_land.at[origin], dq_pair_recv.at[origin])
            total = dq_acc[origin, core] + dq_land[origin]
            dq_out[origin] = total.T.astype(BF16)
            start(*dq_copy(origin))

        def last(pair, carry):
            for place in (2 * pair, 2 * pair + 1):
                for slot in range(LATE):
                    compute(late[slot], slot, chip_at(place), False)
            for place in (2 * pair, 2 * pair + 1):
                move(*dq_pair_copy(chip_at(place))).start()

            @pl.when(pair > 0)
            def _():
                finish_query(2 * pair - 2)
                finish_query(2 * pair - 1)

            return carry

        lax.fori_loop(0, CHIPS // 2, last, 0)
        for slot in range(LATE):
            close_keys(late[slot], slot)
        finish_query(CHIPS - 2)
        finish_query(CHIPS - 1)

    for h in range(HEADS):
        columns = slice(h * WIDTH, (h + 1) * WIDTH)
        landed(rdkv.at[h], dkv_recv.at[h])
        kg_ref[:, columns] = rdkv[h, 0]
        vg_ref[:, columns] = rdkv[h, 1]
    outputs = [
        pltpu.make_async_copy(src, dst, out_sems.at[index])
        for index, (src, dst) in enumerate(((qg_ref, q_out), (kg_ref, k_out), (vg_ref, v_out)))
    ]
    outputs[1].start()
    outputs[2].start()
    inputs[5].wait()
    for m in range(3):
        projected_turned[m] = all_rows(0, m).astype(F32).T.astype(BF16)

    grads_out = (qg_ref, kg_ref, vg_ref)
    order = (1, 2, 0)

    def pair_copy(m):
        return move(pair_send.at[m], pair_land.at[m], pair_sems.at[0, m], pair_sems.at[1, m], twin)

    def sum_copy(m, other):
        return move(
            sum_send.at[m, other], sum_land.at[m, chip],
            sum_sems.at[0, m, other], sum_sems.at[1, m, chip], 2 * other + core,
        )

    def total_copy(m, other):
        return move(
            totals.at[core, m, chip], totals.at[core, m, chip],
            total_sems.at[0, m, other], total_sems.at[1, m, chip], 2 * other + core,
        )

    def twin_copy(m):
        return move(
            totals.at[core, m], totals.at[core, m], twin_sems.at[0, m], twin_sems.at[1, m], twin
        )

    def to_chips(copy, m):
        def one(step, carry):
            copy(m, chip_at(step)).start()
            return carry

        lax.fori_loop(1, CHIPS, one, 0)

    def from_chips(land, sems, m):
        def one(step, carry):
            other = chip_at(step)
            landed(land.at[m, other], sems.at[1, m, other])
            return carry

        lax.fori_loop(1, CHIPS, one, 0)

    def gather_rows(m):
        split_rows(1, m, nt(grads_out[m][...], up_here[m]))

    def up_rows(m):
        rows = nn(projected_turned[m], grads_out[m][...]) * adapter_scale
        for h in range(HEADS):
            partial[m, h * WIDTH : (h + 1) * WIDTH] = rows[:, h * WIDTH : (h + 1) * WIDTH]

        @pl.when(core == 1)
        def _():
            pair_send[m] = partial[m].astype(BF16)
            pair_copy(m).start()

    def row_copy(m):
        return move(
            row_all.at[1, m], row_twin.at[m], row_twin_sems.at[0, m], row_twin_sems.at[1, m], twin
        )

    def to_sums(m, rows):
        sum_send[m] = rows.astype(BF16).reshape(CHIPS, PIECE, WIDTH)
        to_chips(sum_copy, m)
        sum_land[m, chip] = sum_send[m, chip]

    def up_sum(m):
        pair_copy(m).wait_recv()
        to_sums(m, partial[m] + pair_land[m].astype(F32))

    def down_sum(m):
        rows = nn(f_turned[...], all_rows(1, m))
        row_copy(m).wait_recv()
        rows += nn(f_twin[...], row_twin[m].reshape(TOKENS, WIDTH))
        to_sums(m, rows * adapter_scale)

    for m in order[:2]:
        gather_rows(m)
    for h in range(HEADS):
        landed(rdq.at[h], dq_recv.at[h])
        qg_ref[:, h * WIDTH : (h + 1) * WIDTH] = rdq[h]
    outputs[0].start()
    gather_rows(0)
    for m in order:
        up_rows(m)
    for m in order:
        sum_rows(1, m)

    @pl.when(core == 0)
    def _up_sums():
        for m in order:
            up_sum(m)
        for m in order:
            from_heads(1, 1, m)
            row_copy(m).start()

    @pl.when(core == 1)
    def _down_sums():
        f_copy.wait_recv()
        for m in order:
            down_sum(m)

    for m in order:
        from_chips(sum_land, sum_sems, m)
        totals[core, m, chip] = jnp.sum(sum_land[m].astype(F32), axis=0).astype(BF16)
        to_chips(total_copy, m)
    for m in order:
        from_chips(totals.at[core], total_sems, m)
        twin_copy(m).start()
    for m in order:
        landed(totals.at[1 - core, m], twin_sems.at[1, m])

    for copy in outputs:
        copy.wait()
    for m in range(3):
        for kind in range(2):
            for phase in range(2):
                drain_heads(kind, phase, m)
        twin_copy(m).wait_send()

        def drain_chips(step, carry):
            sum_copy(m, chip_at(step)).wait_send()
            total_copy(m, chip_at(step)).wait_send()
            return carry

        lax.fori_loop(1, CHIPS, drain_chips, 0)

    @pl.when(core == 0)
    def _drain_rows():
        f_copy.wait_send()
        for m in range(3):
            row_copy(m).wait_send()

    @pl.when(core == 1)
    def _drain_pairs():
        for m in range(3):
            pair_copy(m).wait_send()

    def drain_sends(h, carry):
        for copy in query_copies(h) + stats_copies(h) + key_copies(h):
            sent(*copy)
        return carry

    lax.fori_loop(0, HEADS, drain_sends, 0)

    @pl.when(working)
    def _drain_work():
        def one(origin, carry):
            for copy in pass_copies(origin) + (dq_pair_copy(origin),):
                move(*copy).wait_send()
            sent(*dq_copy(origin))
            sent(*dkv_copy(origin))
            return carry

        lax.fori_loop(0, CHIPS, one, 0)


def finish_kernel(
    q_in, k_in, v_in, totals, q_out, k_out, v_out, down_out, up_out, down_here, up_here, sems
):
    def leave(index, src, dst):
        copy = pltpu.make_async_copy(src, dst, sems.at[index])
        copy.start()
        return copy

    copies = [
        leave(index, src, dst)
        for index, (src, dst) in enumerate(((q_in, q_out), (k_in, k_out), (v_in, v_out)))
    ]
    for m in range(3):
        down_here[m] = totals[1, m].astype(F32)
        copies.append(leave(3 + m, down_here.at[m], down_out.at[m]))
    for m in range(3):
        for h in range(HEADS):
            columns = slice(h * WIDTH, (h + 1) * WIDTH)
            up_here[m, :, columns] = totals[0, m, columns, :].astype(F32)
        copies.append(leave(6 + m, up_here.at[m], up_out.at[m]))
    for copy in copies:
        copy.wait()


def finish(query_grad, key_grad, value_grad, totals):
    rows = jax.ShapeDtypeStruct(query_grad.shape, BF16)
    vmem = pl.BlockSpec(memory_space=pltpu.VMEM)
    return pl.pallas_call(
        finish_kernel,
        out_shape=(
            rows, rows, rows,
            jax.ShapeDtypeStruct((3, HEADS * WIDTH, WIDTH), F32),
            jax.ShapeDtypeStruct((3, WIDTH, HEADS * WIDTH), F32),
        ),
        in_specs=[vmem] * 4,
        out_specs=(pl.BlockSpec(memory_space=pltpu.HBM),) * 5,
        scratch_shapes=[
            pltpu.VMEM((3, HEADS * WIDTH, WIDTH), F32),
            pltpu.VMEM((3, WIDTH, HEADS * WIDTH), F32),
            pltpu.SemaphoreType.DMA((9,)),
        ],
        compiler_params=pltpu.CompilerParams(vmem_limit_bytes=60 * 2**20),
        name="finish",
    )(query_grad, key_grad, value_grad, totals.reshape(2, 3, HEADS * WIDTH, WIDTH))


def on_device(
    queries,
    key_matrix_rows,
    value_matrix_rows,
    attention_output,
    output_gradient,
    log_sum_norm,
    features,
    adapter_down_weight,
    adapter_up_weight,
    attended_key_blocks,
    used_block_count,
):
    vmem = pl.BlockSpec(memory_space=pltpu.VMEM)
    smem = pl.BlockSpec(memory_space=pltpu.SMEM)
    rows = jax.ShapeDtypeStruct((TOKENS, HEADS * WIDTH), BF16)
    totals = jax.ShapeDtypeStruct((2, 3, CHIPS, PIECE, WIDTH), BF16)
    dma = pltpu.SemaphoreType.DMA
    results = pl.pallas_call(
        layer_kernel,
        out_shape=(rows, rows, rows, totals),
        in_specs=[pl.BlockSpec(memory_space=pltpu.HBM)] * 9 + [smem] * 2,
        out_specs=(pl.BlockSpec(memory_space=pltpu.HBM),) * 3 + (vmem,),
        scratch_shapes=[
            pltpu.VMEM((TOKENS, HEADS * WIDTH), BF16),
            pltpu.VMEM((TOKENS, HEADS * WIDTH), BF16),
            pltpu.VMEM((TOKENS, HEADS * WIDTH), BF16),
            dma((3,)),
            pltpu.VMEM((TOKENS, HEADS * WIDTH), BF16),
            pltpu.VMEM((TOKENS, HEADS * WIDTH), BF16),
            pltpu.VMEM((HEADS, TOKENS), F32),
            pltpu.VMEM((TOKENS, HEADS * WIDTH), BF16),
            pltpu.VMEM((3, HEADS * WIDTH, WIDTH), BF16),
            pltpu.VMEM((3, WIDTH, HEADS * WIDTH), BF16),
            dma((6,)),
            pltpu.VMEM((HEADS, 4, TOKENS), F32),
            pltpu.VMEM((CHIPS, 2, 4, TOKENS), F32),
            pltpu.VMEM((CHIPS, 2, 2, TOKENS, WIDTH), BF16),
            pltpu.VMEM((CHIPS, 2, TOKENS, WIDTH), BF16),
            pltpu.VMEM((EARLY, WIDTH, TOKENS), BF16),
            pltpu.VMEM((EARLY, TOKENS, WIDTH), F32),
            pltpu.VMEM((EARLY, TOKENS, WIDTH), F32),
            pltpu.VMEM((CHIPS, 2, WIDTH, TOKENS), F32),
            pltpu.VMEM((CHIPS, WIDTH, TOKENS), F32),
            pltpu.VMEM((CHIPS, TOKENS, WIDTH), BF16),
            pltpu.VMEM((CHIPS, 2, TOKENS, WIDTH), BF16),
            pltpu.VMEM((HEADS, TOKENS, WIDTH), BF16),
            pltpu.VMEM((HEADS, 2, TOKENS, WIDTH), BF16),
            dma((HEADS,)), dma((2, HEADS)), dma((2, HEADS)), dma((2, CHIPS)),
            dma((CHIPS,)), dma((CHIPS,)), dma((CHIPS,)),
            dma((CHIPS,)), dma((CHIPS,)), dma((CHIPS,)), dma((2, CHIPS)),
            dma((CHIPS,)), dma((HEADS,)), dma((HEADS,)),
            pltpu.VMEM((HEADS * WIDTH, TOKENS), BF16),
            pltpu.VMEM((HEADS * WIDTH, TOKENS), BF16),
            pltpu.VMEM((3, WIDTH, TOKENS), BF16),
            pltpu.VMEM((3, GROUPS, SHARE, WIDTH), BF16),
            dma((2, 3)), dma((2,)),
            pltpu.VMEM((2, 3, GROUPS, SHARE, WIDTH), BF16),
            pltpu.VMEM((2, 3, GROUPS, SHARE, WIDTH), BF16),
            pltpu.VMEM((2, 3, GROUPS, SHARE, WIDTH), BF16),
            dma((2, 2, 2, 3, GROUPS)),
            pltpu.VMEM((3, HEADS * WIDTH, WIDTH), F32),
            pltpu.VMEM((3, HEADS * WIDTH, WIDTH), BF16),
            pltpu.VMEM((3, HEADS * WIDTH, WIDTH), BF16),
            pltpu.VMEM((3, CHIPS, PIECE, WIDTH), BF16),
            pltpu.VMEM((3, CHIPS, PIECE, WIDTH), BF16),
            dma((2, 3)), dma((2, 3, CHIPS)), dma((2, 3, CHIPS)), dma((2, 3)),
        ],
        compiler_params=pltpu.CompilerParams(
            collective_id=0, has_side_effects=True, vmem_limit_bytes=60 * 2**20
        ),
        name="layer",
    )(
        queries, key_matrix_rows, value_matrix_rows, attention_output, output_gradient,
        log_sum_norm, features, adapter_down_weight, adapter_up_weight,
        attended_key_blocks, used_block_count,
    )
    return finish(*results)


def solution(mesh):
    placed = (
        P("ctx", "head"),
        P("ctx", "head"),
        P("ctx", "head"),
        P("ctx", "head"),
        P("ctx", "head"),
        P("head", "ctx"),
        P("ctx", "head"),
        P(None, "head", None),
        P(None, None, "head"),
        P("ctx", None),
        P("ctx"),
    )
    return jax.shard_map(
        on_device,
        mesh=mesh,
        in_specs=placed,
        out_specs=(
            P("ctx", "head"),
            P("ctx", "head"),
            P("ctx", "head"),
            P(None, "head", None),
            P(None, None, "head"),
        ),
        check_vma=False,
    )
```

```python
import functools
import math

import jax
import jax.numpy as jnp
from jax import lax
from jax.experimental import pallas as pl
from jax.experimental.pallas import tpu as pltpu
from jax.sharding import PartitionSpec as P

MESH = pl.DeviceIdType.MESH
BF16 = jnp.bfloat16
F32 = jnp.float32

HEADS = 5
WIDTH = 128
TOKENS = 256
RING = 16
BLOCK = 128
EARLY = 4
LATE = 1
GROUPS = 8
SHARE = TOKENS // GROUPS
CHIPS = RING // 2
PIECE = HEADS * WIDTH // CHIPS
SCALE = WIDTH ** -0.5
LOG2E = math.log2(math.e)
DEAD = 1e30
adapter_scale = 0.125


def nt(a, b):
    return lax.dot_general(a, b, (((1,), (1,)), ((), ())), preferred_element_type=F32)


def nn(a, b):
    return lax.dot_general(a, b, (((1,), (0,)), ((), ())), preferred_element_type=F32)


def lane_slice(h):
    return pl.ds(pl.multiple_of(h * WIDTH, WIDTH), WIDTH)


def tn(a, b):
    return lax.dot_general(a, b, (((0,), (0,)), ((), ())), preferred_element_type=F32)


def layer_kernel(
    q_ref, k_ref, v_ref, o_ref, g_ref, lse_ref, f_ref, down_ref, up_ref, att_ref, used_ref,
    q_out, k_out, v_out, totals,
    qg_ref, kg_ref, vg_ref, out_sems,
    o_here, g_here, lse_here, f_here, down_here, up_here, in_sems,
    stats, rs, rqg, rkv, keys_t, dk_acc, dv_acc, dq_acc, dq_land, dq_out, dkv_out, rdq, rdkv,
    s_send, qg_send, kv_send, pass_send, dq_pair_send, dq_send, dkv_send,
    s_recv, qg_recv, kv_recv, pass_recv, dq_pair_recv, dq_recv, dkv_recv,
    f_turned, f_twin, projected_turned, row_twin, row_twin_sems, f_twin_sems, row_send, row_land, row_all, row_sems,
    partial, pair_send, pair_land, sum_send, sum_land, pair_sems, sum_sems, total_sems, twin_sems,
):
    me = lax.axis_index("ctx")
    group = lax.axis_index("head")
    chip = me // 2
    core = lax.rem(me, 2)
    twin = me + 1 - 2 * core

    def chip_at(step):
        return lax.rem(chip + step, CHIPS)

    def move(src, dst, send_sem, recv_sem, target):
        return pltpu.make_async_remote_copy(
            src_ref=src, dst_ref=dst, send_sem=send_sem, recv_sem=recv_sem,
            device_id=(target, group), device_id_type=MESH,
        )

    def start(src, dst, send_sem, recv_sem, target):
        @pl.when(target != me)
        def _():
            move(src, dst, send_sem, recv_sem, target).start()

        @pl.when(target == me)
        def _():
            pltpu.make_async_copy(src, dst, recv_sem).start()

    def sent(src, dst, send_sem, recv_sem, target):
        @pl.when(target != me)
        def _():
            move(src, dst, send_sem, recv_sem, target).wait_send()

    def landed(dst, recv_sem):
        pltpu.make_async_copy(dst, dst, recv_sem).wait()

    barrier = pltpu.get_barrier_semaphore()

    def greet(step, carry):
        pl.semaphore_signal(
            barrier, inc=1, device_id=(2 * chip_at(step) + core, group), device_id_type=MESH
        )
        return carry

    def greet_head(step, carry):
        pl.semaphore_signal(
            barrier, inc=1, device_id=(me, lax.rem(group + step, GROUPS)), device_id_type=MESH
        )
        return carry

    pl.semaphore_signal(barrier, inc=1, device_id=(twin, group), device_id_type=MESH)
    lax.fori_loop(1, CHIPS, greet, 0)
    lax.fori_loop(1, GROUPS, greet_head, 0)

    inputs = [
        pltpu.make_async_copy(src, dst, in_sems.at[index])
        for index, (src, dst) in enumerate(
            (
                (g_ref, g_here), (o_ref, o_here), (lse_ref, lse_here),
                (f_ref, f_here), (down_ref, down_here), (up_ref, up_here),
            )
        )
    ]
    for copy in inputs:
        copy.start()

    pl.semaphore_wait(barrier, CHIPS + GROUPS - 1)

    def query_copies(h):
        target = 2 * lax.rem(5 * h, CHIPS) + core
        lanes = lane_slice(h)
        return (
            (q_ref.at[:, lanes], rqg.at[chip, core, 0], qg_send.at[0, h], qg_recv.at[chip], target),
            (g_ref.at[:, lanes], rqg.at[chip, core, 1], qg_send.at[1, h], qg_recv.at[chip], target),
        )

    def stats_copies(h):
        target = 2 * lax.rem(5 * h, CHIPS) + core
        return ((stats.at[h], rs.at[chip, core], s_send.at[h], s_recv.at[chip], target),)

    def key_copies(h):
        target = 2 * lax.rem(5 * h, CHIPS) + core
        lanes = lane_slice(h)
        return (
            (k_ref.at[:, lanes], rkv.at[chip, 0], kv_send.at[0, h], kv_recv.at[chip], target),
            (v_ref.at[:, lanes], rkv.at[chip, 1], kv_send.at[1, h], kv_recv.at[chip], target),
        )

    def send_some(copies, begin, end):
        def one(step, carry):
            h = lax.rem(5 * lax.rem(chip - step + CHIPS, CHIPS), CHIPS)

            @pl.when(h < HEADS)
            def _():
                for copy in copies(h):
                    start(*copy)

            return carry

        lax.fori_loop(begin, end, one, 0)

    send_some(key_copies, 0, EARLY)
    send_some(query_copies, 0, CHIPS)

    lane = lax.broadcasted_iota(jnp.int32, (1, TOKENS), 1)
    words = [[jnp.int32(0), jnp.int32(0)], [jnp.int32(0), jnp.int32(0)]]
    for row in range(2):
        for slot in range(16):
            block = att_ref[row, slot]
            owner = jnp.right_shift(block, 1)
            bit = jnp.left_shift(jnp.int32(1), jnp.right_shift(block, 2) * 2 + (block & 1))
            for part in range(2):
                inside = ((owner & 1) == part) & (slot < used_ref[row])
                words[part][row] = words[part][row] | jnp.where(inside, bit, 0)
    codes = [
        jnp.where(lane < TOKENS // 2, word[0], word[1]).astype(F32) for word in words
    ]
    for copy in inputs[:3]:
        copy.wait()
    for h in range(HEADS):
        columns = slice(h * WIDTH, (h + 1) * WIDTH)
        product = g_here[:, columns].astype(F32) * o_here[:, columns].astype(F32)
        row_dot = jnp.sum(product.T, axis=0, keepdims=True)
        norm = lse_here[h : h + 1, :] * LOG2E
        stats[h] = jnp.concatenate(
            [norm, row_dot, codes[0], codes[1]], axis=0
        )

    send_some(stats_copies, 0, CHIPS)
    send_some(key_copies, EARLY, CHIPS)

    def head_copy(kind, phase, m, other):
        if phase == 0:
            src, dst = row_send.at[kind, m, other], row_land.at[kind, m, group]
        else:
            src, dst = row_all.at[kind, m, group], row_all.at[kind, m, group]
        return pltpu.make_async_remote_copy(
            src_ref=src, dst_ref=dst,
            send_sem=row_sems.at[kind, phase, 0, m, other],
            recv_sem=row_sems.at[kind, phase, 1, m, group],
            device_id=(me, other), device_id_type=MESH,
        )

    def to_heads(kind, phase, m):
        def one(step, carry):
            head_copy(kind, phase, m, lax.rem(group + step, GROUPS)).start()
            return carry

        lax.fori_loop(1, GROUPS, one, 0)

    def from_heads(kind, phase, m):
        def one(step, carry):
            other = lax.rem(group + step, GROUPS)
            dst = (row_land if phase == 0 else row_all).at[kind, m, other]
            landed(dst, row_sems.at[kind, phase, 1, m, other])
            return carry

        lax.fori_loop(1, GROUPS, one, 0)

    def drain_heads(kind, phase, m):
        def one(step, carry):
            head_copy(kind, phase, m, lax.rem(group + step, GROUPS)).wait_send()
            return carry

        lax.fori_loop(1, GROUPS, one, 0)

    def split_rows(kind, m, rows):
        row_send[kind, m] = rows.astype(BF16).reshape(GROUPS, SHARE, WIDTH)
        to_heads(kind, 0, m)

    def sum_rows(kind, m):
        row_land[kind, m, group] = row_send[kind, m, group]
        from_heads(kind, 0, m)
        row_all[kind, m, group] = jnp.sum(row_land[kind, m].astype(F32), axis=0).astype(BF16)
        to_heads(kind, 1, m)

    def all_rows(kind, m):
        from_heads(kind, 1, m)
        return row_all[kind, m].reshape(TOKENS, WIDTH)

    inputs[3].wait()
    inputs[4].wait()
    for m in range(3):
        split_rows(0, m, nn(f_here[...], down_here[m]))
    f_turned[...] = f_here[...].astype(F32).T.astype(BF16)
    f_copy = move(f_turned, f_twin, f_twin_sems.at[0], f_twin_sems.at[1], twin)

    @pl.when(core == 0)
    def _():
        f_copy.start()

    my_head = lax.rem(5 * chip, CHIPS)
    working = my_head < HEADS

    def pass_copies(origin):
        return (
            (rs.at[origin, core], rs.at[origin, core],
             pass_send.at[0, origin], pass_recv.at[0, origin], twin),
            (rqg.at[origin, core], rqg.at[origin, core],
             pass_send.at[1, origin], pass_recv.at[1, origin], twin),
        )

    def dq_pair_copy(origin):
        return (dq_acc.at[origin, 1 - core], dq_land.at[origin],
                dq_pair_send.at[origin], dq_pair_recv.at[origin], twin)

    def dq_copy(origin):
        return (dq_out.at[origin], rdq.at[my_head],
                dq_send.at[origin], dq_recv.at[my_head], 2 * origin + core)

    def dkv_copy(origin):
        return (dkv_out.at[origin], rdkv.at[my_head],
                dkv_send.at[origin], dkv_recv.at[my_head], 2 * origin + core)

    def compute(key_chip, slot, origin, first):
        keys = rkv[key_chip, 0]
        queries = rqg[origin, :, 0].reshape(2 * TOKENS, WIDTH)
        grads = rqg[origin, :, 1].reshape(2 * TOKENS, WIDTH)
        norm = jnp.concatenate([rs[origin, side, 0:1, :] for side in range(2)], axis=1)
        row_dot = jnp.concatenate([rs[origin, side, 1:2, :] for side in range(2)], axis=1)
        code = jnp.concatenate(
            [
                jnp.where(core == 0, rs[origin, side, 2:3, :], rs[origin, side, 3:4, :])
                for side in range(2)
            ],
            axis=1,
        ).astype(jnp.int32)
        scores = nt(keys, queries)
        value_dot = nt(rkv[key_chip, 1], grads)
        low_parts, grad_parts = [], []
        for sub in range(2):
            bit = jnp.right_shift(code, key_chip * 2 + sub) & 1
            bias = jnp.where(bit > 0, norm, DEAD)
            piece = slice(sub * BLOCK, (sub + 1) * BLOCK)
            weights = jnp.exp2(scores[piece] * (SCALE * LOG2E) - bias)
            low_parts.append(weights.astype(BF16))
            grad_parts.append(
                (weights * ((value_dot[piece] - row_dot) * SCALE)).astype(BF16)
            )
        low = jnp.concatenate(low_parts, axis=0)
        score_grad = jnp.concatenate(grad_parts, axis=0)
        dv_acc[slot] += nn(low, grads)
        dk_acc[slot] += nn(score_grad, queries)
        dq_part = nn(keys_t[slot], score_grad)
        for side in range(2):
            piece = dq_part[:, side * TOKENS : (side + 1) * TOKENS]
            if first:
                dq_acc[origin, side] = piece
            else:
                dq_acc[origin, side] += piece

    def open_keys(key_chip, slot):
        landed(rkv.at[key_chip], kv_recv.at[key_chip])
        keys_t[slot] = rkv[key_chip, 0].astype(F32).T.astype(BF16)
        dk_acc[slot] = jnp.zeros((TOKENS, WIDTH), F32)
        dv_acc[slot] = jnp.zeros((TOKENS, WIDTH), F32)

    def close_keys(key_chip, slot):
        dkv_out[key_chip, 0] = dk_acc[slot].astype(BF16)
        dkv_out[key_chip, 1] = dv_acc[slot].astype(BF16)
        start(*dkv_copy(key_chip))

    @pl.when(working)
    def _first_keys():
        def receive(step):
            origin = chip_at(step)
            landed(rs.at[origin, core], s_recv.at[origin])
            landed(rqg.at[origin, core], qg_recv.at[origin])
            for copy in pass_copies(origin):
                move(*copy).start()

        def use(step):
            origin = chip_at(step)
            landed(rs.at[origin, 1 - core], pass_recv.at[0, origin])
            landed(rqg.at[origin, 1 - core], pass_recv.at[1, origin])
            for slot in range(EARLY):
                compute(chip_at(slot), slot, origin, slot == 0)

        for slot in range(EARLY):
            open_keys(chip_at(slot), slot)
        receive(0)

        def both(step, carry):
            @pl.when(step < CHIPS)
            def _():
                receive(step)

            @pl.when(step == 5)
            def _():
                for m in range(3):
                    sum_rows(0, m)

            use(step - 1)
            return carry

        lax.fori_loop(1, CHIPS + 1, both, 0)
        for slot in range(EARLY):
            close_keys(chip_at(slot), slot)

    @pl.when(my_head >= HEADS)
    def _idle():
        for m in range(3):
            sum_rows(0, m)

    @pl.when(working)
    def _other_keys():
        def middle(turn, carry):
            key_chip = chip_at(turn)
            open_keys(key_chip, 0)

            def one(step, inner):
                compute(key_chip, 0, chip_at(step), False)
                return inner

            lax.fori_loop(0, CHIPS, one, 0, unroll=CHIPS)
            close_keys(key_chip, 0)
            return carry

        lax.fori_loop(EARLY, CHIPS - LATE, middle, 0)

        late = [chip_at(CHIPS - LATE + slot) for slot in range(LATE)]
        for slot in range(LATE):
            open_keys(late[slot], slot)

        def finish_query(step):
            origin = chip_at(step)
            landed(dq_land.at[origin], dq_pair_recv.at[origin])
            total = dq_acc[origin, core] + dq_land[origin]
            dq_out[origin] = total.T.astype(BF16)
            start(*dq_copy(origin))

        def last(pair, carry):
            for place in (2 * pair, 2 * pair + 1):
                for slot in range(LATE):
                    compute(late[slot], slot, chip_at(place), False)
            for place in (2 * pair, 2 * pair + 1):
                move(*dq_pair_copy(chip_at(place))).start()

            @pl.when(pair > 0)
            def _():
                finish_query(2 * pair - 2)
                finish_query(2 * pair - 1)

            return carry

        lax.fori_loop(0, CHIPS // 2, last, 0)
        for slot in range(LATE):
            close_keys(late[slot], slot)
        finish_query(CHIPS - 2)
        finish_query(CHIPS - 1)

    for h in range(HEADS):
        columns = slice(h * WIDTH, (h + 1) * WIDTH)
        landed(rdkv.at[h], dkv_recv.at[h])
        kg_ref[:, columns] = rdkv[h, 0]
        vg_ref[:, columns] = rdkv[h, 1]
    outputs = [
        pltpu.make_async_copy(src, dst, out_sems.at[index])
        for index, (src, dst) in enumerate(((qg_ref, q_out), (kg_ref, k_out), (vg_ref, v_out)))
    ]
    outputs[1].start()
    outputs[2].start()
    inputs[5].wait()
    for m in range(3):
        projected_turned[m] = all_rows(0, m).astype(F32).T.astype(BF16)

    grads_out = (qg_ref, kg_ref, vg_ref)
    order = (1, 2, 0)

    def pair_copy(m):
        return move(pair_send.at[m], pair_land.at[m], pair_sems.at[0, m], pair_sems.at[1, m], twin)

    def sum_copy(m, other):
        return move(
            sum_send.at[m, other], sum_land.at[m, chip],
            sum_sems.at[0, m, other], sum_sems.at[1, m, chip], 2 * other + core,
        )

    def total_copy(m, other):
        return move(
            totals.at[core, m, chip], totals.at[core, m, chip],
            total_sems.at[0, m, other], total_sems.at[1, m, chip], 2 * other + core,
        )

    def twin_copy(m):
        return move(
            totals.at[core, m], totals.at[core, m], twin_sems.at[0, m], twin_sems.at[1, m], twin
        )

    def to_chips(copy, m):
        def one(step, carry):
            copy(m, chip_at(CHIPS - step)).start()
            return carry

        lax.fori_loop(1, CHIPS, one, 0)

    def from_chips(land, sems, m):
        def one(step, carry):
            other = chip_at(step)
            landed(land.at[m, other], sems.at[1, m, other])
            return carry

        lax.fori_loop(1, CHIPS, one, 0)

    def gather_rows(m):
        split_rows(1, m, nt(grads_out[m][...], up_here[m]))

    def up_rows(m):
        rows = nn(projected_turned[m], grads_out[m][...]) * adapter_scale
        for h in range(HEADS):
            partial[m, h * WIDTH : (h + 1) * WIDTH] = rows[:, h * WIDTH : (h + 1) * WIDTH]

        @pl.when(core == 1)
        def _():
            pair_send[m] = partial[m].astype(BF16)
            pair_copy(m).start()

    def row_copy(m):
        return move(
            row_all.at[1, m], row_twin.at[m], row_twin_sems.at[0, m], row_twin_sems.at[1, m], twin
        )

    def to_sums(m, rows):
        sum_send[m] = rows.astype(BF16).reshape(CHIPS, PIECE, WIDTH)
        to_chips(sum_copy, m)
        sum_land[m, chip] = sum_send[m, chip]

    def up_sum(m):
        pair_copy(m).wait_recv()
        to_sums(m, partial[m] + pair_land[m].astype(F32))

    def down_sum(m):
        rows = nn(f_turned[...], all_rows(1, m))
        row_copy(m).wait_recv()
        rows += nn(f_twin[...], row_twin[m].reshape(TOKENS, WIDTH))
        to_sums(m, rows * adapter_scale)

    for m in order[:2]:
        gather_rows(m)
    for m in order[:2]:
        up_rows(m)
    for h in range(HEADS):
        landed(rdq.at[h], dq_recv.at[h])
        qg_ref[:, h * WIDTH : (h + 1) * WIDTH] = rdq[h]
    outputs[0].start()
    gather_rows(0)
    for m in order[:2]:
        sum_rows(1, m)
    up_rows(0)
    sum_rows(1, 0)

    @pl.when(core == 0)
    def _up_sums():
        for m in order:
            up_sum(m)
        for m in order:
            from_heads(1, 1, m)
            row_copy(m).start()

    @pl.when(core == 1)
    def _down_sums():
        f_copy.wait_recv()
        for m in order:
            down_sum(m)

    for m in order:
        from_chips(sum_land, sum_sems, m)
        totals[core, m, chip] = jnp.sum(sum_land[m].astype(F32), axis=0).astype(BF16)
        to_chips(total_copy, m)
    for m in order:
        from_chips(totals.at[core], total_sems, m)
        twin_copy(m).start()
    for m in order:
        landed(totals.at[1 - core, m], twin_sems.at[1, m])

    for copy in outputs:
        copy.wait()
    for m in range(3):
        for kind in range(2):
            for phase in range(2):
                drain_heads(kind, phase, m)
        twin_copy(m).wait_send()

        def drain_chips(step, carry):
            sum_copy(m, chip_at(step)).wait_send()
            total_copy(m, chip_at(step)).wait_send()
            return carry

        lax.fori_loop(1, CHIPS, drain_chips, 0)

    @pl.when(core == 0)
    def _drain_rows():
        f_copy.wait_send()
        for m in range(3):
            row_copy(m).wait_send()

    @pl.when(core == 1)
    def _drain_pairs():
        for m in range(3):
            pair_copy(m).wait_send()

    def drain_sends(h, carry):
        for copy in query_copies(h) + stats_copies(h) + key_copies(h):
            sent(*copy)
        return carry

    lax.fori_loop(0, HEADS, drain_sends, 0)

    @pl.when(working)
    def _drain_work():
        def one(origin, carry):
            for copy in pass_copies(origin) + (dq_pair_copy(origin),):
                move(*copy).wait_send()
            sent(*dq_copy(origin))
            sent(*dkv_copy(origin))
            return carry

        lax.fori_loop(0, CHIPS, one, 0)


def finish_kernel(
    q_in, k_in, v_in, totals, q_out, k_out, v_out, down_out, up_out, down_here, up_here, sems
):
    def leave(index, src, dst):
        copy = pltpu.make_async_copy(src, dst, sems.at[index])
        copy.start()
        return copy

    copies = [
        leave(index, src, dst)
        for index, (src, dst) in enumerate(((q_in, q_out), (k_in, k_out), (v_in, v_out)))
    ]
    for m in range(3):
        down_here[m] = totals[1, m].astype(F32)
        copies.append(leave(3 + m, down_here.at[m], down_out.at[m]))
    for m in range(3):
        for h in range(HEADS):
            columns = slice(h * WIDTH, (h + 1) * WIDTH)
            up_here[m, :, columns] = totals[0, m, columns, :].astype(F32)
        copies.append(leave(6 + m, up_here.at[m], up_out.at[m]))
    for copy in copies:
        copy.wait()


def finish(query_grad, key_grad, value_grad, totals):
    rows = jax.ShapeDtypeStruct(query_grad.shape, BF16)
    vmem = pl.BlockSpec(memory_space=pltpu.VMEM)
    return pl.pallas_call(
        finish_kernel,
        out_shape=(
            rows, rows, rows,
            jax.ShapeDtypeStruct((3, HEADS * WIDTH, WIDTH), F32),
            jax.ShapeDtypeStruct((3, WIDTH, HEADS * WIDTH), F32),
        ),
        in_specs=[vmem] * 4,
        out_specs=(pl.BlockSpec(memory_space=pltpu.HBM),) * 5,
        scratch_shapes=[
            pltpu.VMEM((3, HEADS * WIDTH, WIDTH), F32),
            pltpu.VMEM((3, WIDTH, HEADS * WIDTH), F32),
            pltpu.SemaphoreType.DMA((9,)),
        ],
        compiler_params=pltpu.CompilerParams(vmem_limit_bytes=60 * 2**20),
        name="finish",
    )(query_grad, key_grad, value_grad, totals.reshape(2, 3, HEADS * WIDTH, WIDTH))


def on_device(
    queries,
    key_matrix_rows,
    value_matrix_rows,
    attention_output,
    output_gradient,
    log_sum_norm,
    features,
    adapter_down_weight,
    adapter_up_weight,
    attended_key_blocks,
    used_block_count,
):
    vmem = pl.BlockSpec(memory_space=pltpu.VMEM)
    smem = pl.BlockSpec(memory_space=pltpu.SMEM)
    rows = jax.ShapeDtypeStruct((TOKENS, HEADS * WIDTH), BF16)
    totals = jax.ShapeDtypeStruct((2, 3, CHIPS, PIECE, WIDTH), BF16)
    dma = pltpu.SemaphoreType.DMA
    results = pl.pallas_call(
        layer_kernel,
        out_shape=(rows, rows, rows, totals),
        in_specs=[pl.BlockSpec(memory_space=pltpu.HBM)] * 9 + [smem] * 2,
        out_specs=(pl.BlockSpec(memory_space=pltpu.HBM),) * 3 + (vmem,),
        scratch_shapes=[
            pltpu.VMEM((TOKENS, HEADS * WIDTH), BF16),
            pltpu.VMEM((TOKENS, HEADS * WIDTH), BF16),
            pltpu.VMEM((TOKENS, HEADS * WIDTH), BF16),
            dma((3,)),
            pltpu.VMEM((TOKENS, HEADS * WIDTH), BF16),
            pltpu.VMEM((TOKENS, HEADS * WIDTH), BF16),
            pltpu.VMEM((HEADS, TOKENS), F32),
            pltpu.VMEM((TOKENS, HEADS * WIDTH), BF16),
            pltpu.VMEM((3, HEADS * WIDTH, WIDTH), BF16),
            pltpu.VMEM((3, WIDTH, HEADS * WIDTH), BF16),
            dma((6,)),
            pltpu.VMEM((HEADS, 4, TOKENS), F32),
            pltpu.VMEM((CHIPS, 2, 4, TOKENS), F32),
            pltpu.VMEM((CHIPS, 2, 2, TOKENS, WIDTH), BF16),
            pltpu.VMEM((CHIPS, 2, TOKENS, WIDTH), BF16),
            pltpu.VMEM((EARLY, WIDTH, TOKENS), BF16),
            pltpu.VMEM((EARLY, TOKENS, WIDTH), F32),
            pltpu.VMEM((EARLY, TOKENS, WIDTH), F32),
            pltpu.VMEM((CHIPS, 2, WIDTH, TOKENS), F32),
            pltpu.VMEM((CHIPS, WIDTH, TOKENS), F32),
            pltpu.VMEM((CHIPS, TOKENS, WIDTH), BF16),
            pltpu.VMEM((CHIPS, 2, TOKENS, WIDTH), BF16),
            pltpu.VMEM((HEADS, TOKENS, WIDTH), BF16),
            pltpu.VMEM((HEADS, 2, TOKENS, WIDTH), BF16),
            dma((HEADS,)), dma((2, HEADS)), dma((2, HEADS)), dma((2, CHIPS)),
            dma((CHIPS,)), dma((CHIPS,)), dma((CHIPS,)),
            dma((CHIPS,)), dma((CHIPS,)), dma((CHIPS,)), dma((2, CHIPS)),
            dma((CHIPS,)), dma((HEADS,)), dma((HEADS,)),
            pltpu.VMEM((HEADS * WIDTH, TOKENS), BF16),
            pltpu.VMEM((HEADS * WIDTH, TOKENS), BF16),
            pltpu.VMEM((3, WIDTH, TOKENS), BF16),
            pltpu.VMEM((3, GROUPS, SHARE, WIDTH), BF16),
            dma((2, 3)), dma((2,)),
            pltpu.VMEM((2, 3, GROUPS, SHARE, WIDTH), BF16),
            pltpu.VMEM((2, 3, GROUPS, SHARE, WIDTH), BF16),
            pltpu.VMEM((2, 3, GROUPS, SHARE, WIDTH), BF16),
            dma((2, 2, 2, 3, GROUPS)),
            pltpu.VMEM((3, HEADS * WIDTH, WIDTH), F32),
            pltpu.VMEM((3, HEADS * WIDTH, WIDTH), BF16),
            pltpu.VMEM((3, HEADS * WIDTH, WIDTH), BF16),
            pltpu.VMEM((3, CHIPS, PIECE, WIDTH), BF16),
            pltpu.VMEM((3, CHIPS, PIECE, WIDTH), BF16),
            dma((2, 3)), dma((2, 3, CHIPS)), dma((2, 3, CHIPS)), dma((2, 3)),
        ],
        compiler_params=pltpu.CompilerParams(
            collective_id=0, has_side_effects=True, vmem_limit_bytes=60 * 2**20
        ),
        name="layer",
    )(
        queries, key_matrix_rows, value_matrix_rows, attention_output, output_gradient,
        log_sum_norm, features, adapter_down_weight, adapter_up_weight,
        attended_key_blocks, used_block_count,
    )
    return finish(*results)


def solution(mesh):
    placed = (
        P("ctx", "head"),
        P("ctx", "head"),
        P("ctx", "head"),
        P("ctx", "head"),
        P("ctx", "head"),
        P("head", "ctx"),
        P("ctx", "head"),
        P(None, "head", None),
        P(None, None, "head"),
        P("ctx", None),
        P("ctx"),
    )
    return jax.shard_map(
        on_device,
        mesh=mesh,
        in_specs=placed,
        out_specs=(
            P("ctx", "head"),
            P("ctx", "head"),
            P("ctx", "head"),
            P(None, "head", None),
            P(None, None, "head"),
        ),
        check_vma=False,
    )
```
